32 devices in a mesh: dp: 8 (over y, x, core), seq: 4 (over z).
Axes of the slice: x: 2, y: 2, z: 4, core: 2. Of those that a mesh axis runs over, the one named last changes fastest.
Arguments:
- q_space: bfloat16 [8, 640, 1152], P('dp', 'seq'), may hold values from -64 to 64
- k_space: bfloat16 [8, 640, 1152], P('dp', 'seq'), may hold values from -6 to 6
- v_space: bfloat16 [8, 640, 1152], P('dp', 'seq'), may hold values from -6 to 6
- q_time: bfloat16 [8, 640, 1152], P('dp', 'seq'), may hold values from -64 to 64
- k_time: bfloat16 [8, 640, 1152], P('dp', 'seq'), may hold values from -6 to 6
- v_time: bfloat16 [8, 640, 1152], P('dp', 'seq'), may hold values from -6 to 6
- weight: bfloat16 [1152, 1152], P('dp'), may hold values from -0.1875 to 0.1875
- target: bfloat16 [8, 640, 1152], P('dp', 'seq'), may hold values from -6 to 6
Outputs:
- grad_q_space: bfloat16 [8, 640, 1152], P('dp', 'seq')
- grad_k_space: bfloat16 [8, 640, 1152], P('dp', 'seq')
- grad_v_space: bfloat16 [8, 640, 1152], P('dp', 'seq')
- grad_q_time: bfloat16 [8, 640, 1152], P('dp', 'seq')
- grad_k_time: bfloat16 [8, 640, 1152], P('dp', 'seq')
- grad_v_time: bfloat16 [8, 640, 1152], P('dp', 'seq')
- weight_grad: float32 [1152, 1152], P('seq')
The draws below stay inside these ranges and needn't reach their ends.
All inputs are finite; a program needn't handle non-finite values.
Results may differ from the reference program's by a relative error of at most 0.025.
Values may be sent and summed in bfloat16 or wider, within the bound.
No kernel may reach another device: no remote copies, remote signals or barrier semaphores. Data moves between devices by JAX's collectives and lax.ppermute only.
A program may use at most 64 MiB of HBM per device.

```python
import math
import jax
import jax.numpy as jnp
from jax import lax

D = 1152
HEADS = 16
HEAD_DIM = 72
PATCHES = 160
FRAMES = 4
TOKENS = 640
CLIPS = 8
N_SEQ = 4


def pair_space(base_key):
    folded = jax.random.fold_in(base_key, 101)
    query_key, key_key = jax.random.split(folded, 2)
    layout = (CLIPS, FRAMES, PATCHES, D)
    queries = jnp.clip(jax.random.normal(query_key, layout, jnp.float32), -6.0, 6.0)
    key_data = jnp.clip(jax.random.normal(key_key, layout, jnp.float32), -6.0, 6.0)
    return (queries.reshape(CLIPS, FRAMES * PATCHES, D), key_data.reshape(CLIPS, FRAMES * PATCHES, D))


def pair_time(base_key):
    folded = jax.random.fold_in(base_key, 202)
    query_key, key_key = jax.random.split(folded, 2)
    layout = (CLIPS, FRAMES, PATCHES, D)
    queries = jnp.clip(jax.random.normal(query_key, layout, jnp.float32), -6.0, 6.0)
    key_data = jnp.clip(jax.random.normal(key_key, layout, jnp.float32), -6.0, 6.0)
    return (queries.reshape(CLIPS, FRAMES * PATCHES, D), key_data.reshape(CLIPS, FRAMES * PATCHES, D))


def draw_q_space(key, part):
    return pair_space(key)[0].astype(jnp.bfloat16)


def draw_k_space(key, part):
    return pair_space(key)[1].astype(jnp.bfloat16)


def draw_q_time(key, part):
    return pair_time(key)[0].astype(jnp.bfloat16)


def draw_k_time(key, part):
    return pair_time(key)[1].astype(jnp.bfloat16)


def levels(key, extent, cuts, smallest, largest):
    def one(axis_at, shards_of):
        heights = jax.random.uniform(jax.random.fold_in(jax.random.fold_in(key, 6), axis_at), (shards_of,), jnp.float32, smallest / len(cuts), largest / len(cuts))
        return jnp.repeat(jnp.exp(heights), extent[axis_at] // shards_of).reshape((-1,) + (1,) * (len(extent) - axis_at - 1))

    loudness = one(*cuts[0])
    for cut in cuts[1:]:
        loudness = loudness * one(*cut)
    return loudness


def centred(rng, dims, scale, limit, cuts=(), held_as=jnp.bfloat16):
    drawn = jax.random.normal(rng, dims, jnp.float32) * scale
    if len(cuts) > 0:
        drawn = levels(rng, dims, cuts, -0.22, 0.18) * drawn
    return jnp.clip(drawn, min=-limit, max=limit).astype(held_as)


def setup_inputs(seed: int = 0) -> dict:
    splits = jax.random.split(jax.random.key(seed), 9)
    q_space = draw_q_space(jax.random.fold_in(splits[8], 71), 0)
    k_space = draw_k_space(jax.random.fold_in(splits[8], 71), 0)
    v_space = centred(splits[2], (CLIPS, TOKENS, D), 1.0, 6.0, ((0, 8), (1, 4)))
    q_time = draw_q_time(jax.random.fold_in(splits[8], 71), 0)
    k_time = draw_k_time(jax.random.fold_in(splits[8], 71), 0)
    v_time = centred(splits[5], (CLIPS, TOKENS, D), 1.0, 6.0, ((0, 8), (1, 4)))
    weight = centred(splits[6], (D, D), D ** -0.5, 0.1875, ((0, 8),))
    target = centred(splits[7], (CLIPS, TOKENS, D), 1.0, 6.0, ((0, 8), (1, 4)))
    return {"q_space": q_space, "k_space": k_space, "v_space": v_space, "q_time": q_time, "k_time": k_time, "v_time": v_time, "weight": weight, "target": target}


def form_pair(layout):
    if layout == 'space':
        return ('blhe', 'bmhe')
    return ('lbhe', 'mbhe')

def product(pattern, left, right):
    return jnp.einsum(pattern, left.astype(jnp.float32), right.astype(jnp.float32), precision=lax.Precision.HIGHEST)

def attend_forward(query, key_data, values, layout):
    query_form, key_form = form_pair(layout)
    scaling = 1.0 / math.sqrt(HEAD_DIM)
    logits = product(query_form + ',' + key_form + '->bhlm', query, key_data) * scaling
    row_max = lax.optimization_barrier(jnp.max(logits, axis=-1, keepdims=True))
    lifted = jnp.exp(logits - row_max)
    attention = lifted / lax.optimization_barrier(jnp.sum(lifted, axis=-1, keepdims=True))
    rounded = attention.astype(jnp.bfloat16)
    result = product('bhlm,' + key_form + '->' + query_form, rounded, values)
    return (attention, rounded, result)

def attend_backward(query, key_data, values, attention, rounded, step_grad, layout):
    query_form, key_form = form_pair(layout)
    scaling = 1.0 / math.sqrt(HEAD_DIM)
    upstream = product(query_form + ',' + key_form + '->bhlm', step_grad, values)
    grad_values = product('bhlm,' + query_form + '->' + key_form, rounded, step_grad).astype(jnp.bfloat16)
    grad_scores = (attention * (upstream - lax.optimization_barrier(jnp.sum(attention * upstream, axis=-1, keepdims=True)))).astype(jnp.bfloat16)
    grad_query = (product('bhlm,' + key_form + '->' + query_form, grad_scores, key_data) * scaling).astype(jnp.bfloat16)
    grad_keys = (product('bhlm,' + query_form + '->' + key_form, grad_scores, query) * scaling).astype(jnp.bfloat16)
    return (grad_query, grad_keys, grad_values)

def split_heads(array):
    return array.reshape(FRAMES, PATCHES, HEADS, HEAD_DIM)

def one_clip(weight, arrays):
    space_q, space_k, space_v, time_q, time_k, time_v, target_rows = [split_heads(item) for item in arrays]
    attention_s, rounded_s, result_s = attend_forward(space_q, space_k, space_v, 'space')
    attention_t, rounded_t, result_t = attend_forward(time_q, time_k, time_v, 'time')
    out_space = result_s.astype(jnp.bfloat16)
    combined = (out_space.astype(jnp.float32) + result_t).astype(jnp.bfloat16).reshape(TOKENS, D)
    projected = jnp.dot(combined, weight, preferred_element_type=jnp.float32)
    output_grad = (projected - target_rows.reshape(TOKENS, D).astype(jnp.float32)).astype(jnp.bfloat16)
    step_grad = jnp.dot(output_grad, weight.T, preferred_element_type=jnp.float32).astype(jnp.bfloat16)
    step_heads = split_heads(step_grad)
    grads_space = attend_backward(space_q, space_k, space_v, attention_s, rounded_s, step_heads, 'space')
    grads_time = attend_backward(time_q, time_k, time_v, attention_t, rounded_t, step_heads, 'time')
    blocks = combined.reshape(FRAMES, N_SEQ, PATCHES // N_SEQ, D)
    grad_blocks = output_grad.reshape(FRAMES, N_SEQ, PATCHES // N_SEQ, D)
    partials = product('fnpi,fnpc->nic', blocks, grad_blocks)
    partials_b = lax.optimization_barrier(partials.astype(jnp.bfloat16))
    partial_sum = lax.optimization_barrier(jnp.sum(partials_b.astype(jnp.float32), axis=0))
    outputs = [item.reshape(TOKENS, D) for item in grads_space + grads_time]
    return tuple(outputs) + (partial_sum,)

def reference(q_space, k_space, v_space, q_time, k_time, v_time, weight, target):
    results = lax.map(lambda arrays: one_clip(weight, arrays), (q_space, k_space, v_space, q_time, k_time, v_time, target))
    weight_grad = lax.optimization_barrier(jnp.sum(results[6], axis=0)) * (1.0 / math.sqrt(CLIPS * TOKENS))
    return (results[0], results[1], results[2], results[3], results[4], results[5], weight_grad)
```

```python
import functools
import math

import jax
import jax.numpy as jnp
from jax import lax
from jax.experimental import pallas as pl
from jax.experimental.pallas import tpu as pltpu
from jax.sharding import PartitionSpec as P

HEAD_DIM = 72
LANES = 128
VMEM_BYTES = 24 * 1024 * 1024
F32 = jnp.float32
BF16 = jnp.bfloat16
NT = (((1,), (1,)), ((), ()))
NN = (((1,), (0,)), ((), ()))
TN = (((0,), (0,)), ((), ()))


def dot(left, right, form):
    return lax.dot_general(left, right, form, preferred_element_type=F32)


def windows(width):
    found = []
    for head in range(width // HEAD_DIM):
        first = head * HEAD_DIM
        start = first // LANES * LANES
        size = -(-(first + HEAD_DIM - start) // LANES) * LANES
        found.append((start, size, first - start))
    return found


def head_only(block, offset):
    lane = lax.broadcasted_iota(jnp.int32, (1, block.shape[1]), 1)
    inside = (lane >= offset) & (lane < offset + HEAD_DIM)
    return jnp.where(inside, block, jnp.zeros_like(block))


def same_patch(rows, per_block):
    left = lax.broadcasted_iota(jnp.int32, (rows, 1), 0) % per_block
    right = lax.broadcasted_iota(jnp.int32, (1, rows), 1) % per_block
    return left == right


def forward_kernel(per_block, q_ref, k_ref, v_ref, out_ref, probs_ref, total):
    rows, width = q_ref.shape
    scaling = 1.0 / math.sqrt(HEAD_DIM)
    keep = None if per_block is None else same_patch(rows, per_block)
    total[...] = jnp.zeros_like(total)
    for head, (start, size, offset) in enumerate(windows(width)):
        lanes = slice(start, start + size)
        logits = dot(head_only(q_ref[:, lanes], offset), k_ref[:, lanes], NT) * scaling
        if keep is not None:
            logits = jnp.where(keep, logits, -1e30)
        lifted = jnp.exp(logits - jnp.max(logits, axis=-1, keepdims=True))
        probs = lifted * (1.0 / jnp.sum(lifted, axis=-1, keepdims=True))
        probs_ref[head] = probs
        total[:, lanes] += dot(probs.astype(BF16), head_only(v_ref[:, lanes], offset), NN)
    out_ref[...] = total[...].astype(out_ref.dtype)


def backward_kernel(
    q_ref, k_ref, v_ref, g_ref, probs_ref, dq_ref, dk_ref, dv_ref, dq_sum, dk_sum, dv_sum
):
    scaling = 1.0 / math.sqrt(HEAD_DIM)
    dq_sum[...] = jnp.zeros_like(dq_sum)
    dk_sum[...] = jnp.zeros_like(dk_sum)
    dv_sum[...] = jnp.zeros_like(dv_sum)
    for head, (start, size, offset) in enumerate(windows(q_ref.shape[1])):
        lanes = slice(start, start + size)
        probs = probs_ref[head]
        step = head_only(g_ref[:, lanes], offset)
        upstream = dot(step, v_ref[:, lanes], NT)
        dv_sum[:, lanes] += dot(probs.astype(BF16), step, TN)
        mean = jnp.sum(probs * upstream, axis=-1, keepdims=True)
        dscore = (probs * (upstream - mean)).astype(BF16)
        dq_sum[:, lanes] += dot(dscore, head_only(k_ref[:, lanes], offset), NN)
        dk_sum[:, lanes] += dot(dscore, head_only(q_ref[:, lanes], offset), TN)
    dq_ref[...] = (dq_sum[...] * scaling).astype(BF16)
    dk_ref[...] = (dk_sum[...] * scaling).astype(BF16)
    dv_ref[...] = dv_sum[...].astype(BF16)


def project_kernel(space_ref, time_ref, weight_ref, target_ref, comb_ref, og_ref, step_ref):
    comb = (space_ref[...].astype(F32) + time_ref[...].astype(F32)).astype(BF16)
    comb_ref[...] = comb
    projected = dot(comb, weight_ref[...], NN)
    og = (projected - target_ref[...].astype(F32)).astype(BF16)
    og_ref[...] = og
    step_ref[...] = dot(og, weight_ref[...], NT).astype(BF16)


def call(body, outs, scratch, flops, moved, *args):
    return pl.pallas_call(
        body,
        out_shape=outs,
        scratch_shapes=scratch,
        cost_estimate=pl.CostEstimate(flops=flops, bytes_accessed=moved, transcendentals=0),
        compiler_params=pltpu.CompilerParams(vmem_limit_bytes=VMEM_BYTES),
    )(*args)


def attend_forward(q, k, v, per_block):
    rows, width = q.shape
    heads = width // HEAD_DIM
    return call(
        functools.partial(forward_kernel, per_block),
        (
            jax.ShapeDtypeStruct((rows, width), BF16),
            jax.ShapeDtypeStruct((heads, rows, rows), F32),
        ),
        [pltpu.VMEM((rows, width), F32)],
        4 * 10**9,
        8 * 10**6,
        q,
        k,
        v,
    )


def attend_backward(q, k, v, step, probs):
    rows, width = q.shape
    return call(
        backward_kernel,
        (jax.ShapeDtypeStruct((rows, width), BF16),) * 3,
        [pltpu.VMEM((rows, width), F32)] * 3,
        6 * 10**9,
        8 * 10**6,
        q,
        k,
        v,
        step,
        probs,
    )


def project(space, time, weight, target):
    return call(
        project_kernel,
        (jax.ShapeDtypeStruct(space.shape, BF16),) * 3,
        [],
        3 * 10**9,
        5 * 10**6,
        space,
        time,
        weight,
        target,
    )


def swap(array, axis, bits):
    size = lax.axis_size(axis)
    return lax.ppermute(array, axis, [(i, i ^ bits) for i in range(size)])


def pick(array, index):
    return lax.dynamic_index_in_dim(array, index, 0, keepdims=False)


def in_order(pieces, me):
    stacked = jnp.stack(pieces)
    return jnp.concatenate([pick(stacked, me ^ i) for i in range(len(pieces))], axis=0)


def gather_weight(weight):
    size = lax.axis_size("dp")
    me = lax.axis_index("dp")
    chips = jnp.stack([weight] + [swap(weight, "dp", 2 * i) for i in range(1, size // 2)])
    other = swap(chips, "dp", 1)
    pieces = jnp.stack([chips, other], axis=1).reshape((size,) + weight.shape)
    return jnp.concatenate([pick(pieces, me ^ i) for i in range(size)], axis=0)


def grad_kernel(chip_size, core_ref, chip_ref, comb_ref, og_ref, out_ref, total):
    size = out_ref.shape[-1]
    first = pl.multiple_of(core_ref[0] * (og_ref.shape[-1] - size), LANES)
    term = dot(comb_ref[0], og_ref[0, :, pl.ds(first, size)], TN)
    term += dot(comb_ref[1], og_ref[1, :, pl.ds(first, size)], TN)
    total[...] = term.reshape(total.shape)
    for i in range(chip_size):
        out_ref[i] = total[:, chip_ref[0] ^ i].astype(BF16)


def weight_gradient(comb, og, scaling):
    width = comb.shape[-1]
    chip_size = lax.axis_size("dp") // 2
    groups = lax.axis_size("seq")
    me, seq = lax.axis_index("dp"), lax.axis_index("seq")
    core, chip = me % 2, me // 2
    rows = width // groups // chip_size
    if rows * groups * chip_size != width or rows % 8 != 0:
        term = dot(comb, og, TN).astype(BF16)
        share = lax.psum_scatter(term, "seq", scatter_dimension=0, tiled=True)
        return lax.psum(share, "dp").astype(F32) * scaling
    size = -(-width // (2 * LANES)) * LANES
    pair = jnp.stack([comb, og])
    other = swap(pair, "dp", 1)
    pieces = pl.pallas_call(
        functools.partial(grad_kernel, chip_size),
        out_shape=jax.ShapeDtypeStruct((chip_size, groups, rows, size), BF16),
        in_specs=[pl.BlockSpec(memory_space=pltpu.SMEM)] * 2
        + [pl.BlockSpec(memory_space=pltpu.VMEM)] * 2,
        scratch_shapes=[pltpu.VMEM((groups, chip_size, rows, size), F32)],
        cost_estimate=pl.CostEstimate(flops=3 * 10**9, bytes_accessed=4 * 10**6, transcendentals=0),
        compiler_params=pltpu.CompilerParams(vmem_limit_bytes=VMEM_BYTES),
    )(core.reshape(1), chip.reshape(1), jnp.stack([comb, other[0]]), jnp.stack([og, other[1]]))
    share = pieces[0].astype(F32)
    for i in range(1, chip_size):
        share += swap(pieces[i], "dp", 2 * i).astype(F32)
    share = share.astype(BF16)
    total = pick(share, seq).astype(F32)
    for i in range(1, groups):
        total += swap(pick(share, seq ^ i), "seq", i).astype(F32)
    total = total.astype(BF16)
    mine = in_order([total] + [swap(total, "dp", 2 * i) for i in range(1, chip_size)], chip)
    other = swap(mine, "dp", 1)
    low = jnp.where(core == 0, mine, other)
    high = jnp.where(core == 0, other, mine)
    whole = jnp.concatenate([low, high[:, 2 * size - width :]], axis=1)
    return whole.astype(F32) * scaling


def shards(q_space, k_space, v_space, q_time, k_time, v_time, weight, target):
    groups = lax.axis_size("seq")
    me = lax.axis_index("seq")
    rows, width = q_space.shape[1:]
    per_block = rows // groups
    home = (rows, width)

    def block(array, index):
        return lax.dynamic_slice_in_dim(array, index * per_block, per_block, axis=-2)

    times = [item.reshape(home) for item in (q_time, k_time, v_time)]
    sent = [jnp.stack([block(item, me ^ i) for item in times]) for i in range(groups)]
    there = [sent[0]] + [swap(sent[i], "seq", i) for i in range(1, groups)]
    time_q, time_k, time_v = jnp.concatenate(there, axis=1)
    full_weight = gather_weight(weight)
    space_q, space_k, space_v = [item.reshape(home) for item in (q_space, k_space, v_space)]
    out_space, probs_s = attend_forward(space_q, space_k, space_v, None)
    out_time, probs_t = attend_forward(time_q, time_k, time_v, per_block)

    def come_home(array):
        parts = array.reshape(array.shape[:-2] + (groups, per_block, width))
        parts = [parts[..., i, :, :] for i in range(groups)]
        return [parts[0]] + [swap(parts[i], "seq", i) for i in range(1, groups)]

    time_home = in_order(come_home(out_time), me)
    comb, og, step = project(out_space, time_home, full_weight, target.reshape(home))
    step_there = jnp.concatenate(
        [block(step, me)] + [swap(block(step, me ^ i), "seq", i) for i in range(1, groups)]
    )
    time_grads = attend_backward(time_q, time_k, time_v, step_there, probs_t)
    back = [in_order(come_home(item), me) for item in time_grads]
    space_grads = attend_backward(space_q, space_k, space_v, step, probs_s)
    scaling = 1.0 / math.sqrt(lax.axis_size("dp") * groups * rows)
    weight_grad = weight_gradient(comb, og, scaling)
    outs = [item.reshape(q_space.shape) for item in list(space_grads) + back]
    return tuple(outs) + (weight_grad,)


def solution(mesh):
    tokens = P("dp", "seq", None)
    return jax.shard_map(
        shards,
        mesh=mesh,
        in_specs=(tokens,) * 6 + (P("dp", None), tokens),
        out_specs=(tokens,) * 6 + (P("seq", None),),
        check_vma=False,
    )
```

```python
import functools
import math

import jax
import jax.numpy as jnp
from jax import lax
from jax.experimental import pallas as pl
from jax.experimental.pallas import tpu as pltpu
from jax.sharding import PartitionSpec as P

HEAD_DIM = 72
LANES = 128
VMEM_BYTES = 24 * 1024 * 1024
COST = 10**10
SMALL = 10
F32 = jnp.float32
BF16 = jnp.bfloat16
NT = (((1,), (1,)), ((), ()))
NN = (((1,), (0,)), ((), ()))
TN = (((0,), (0,)), ((), ()))


def dot(left, right, form):
    return lax.dot_general(left, right, form, preferred_element_type=F32)


def windows(width):
    found = []
    for head in range(width // HEAD_DIM):
        first = head * HEAD_DIM
        start = first // LANES * LANES
        size = -(-(first + HEAD_DIM - start) // LANES) * LANES
        found.append((start, size, first - start))
    return found


def head_only(block, offset):
    lane = lax.broadcasted_iota(jnp.int32, (1, block.shape[1]), 1)
    inside = (lane >= offset) & (lane < offset + HEAD_DIM)
    return jnp.where(inside, block, jnp.zeros_like(block))


def same_patch(rows, per_block):
    left = lax.broadcasted_iota(jnp.int32, (rows, 1), 0) % per_block
    right = lax.broadcasted_iota(jnp.int32, (1, rows), 1) % per_block
    return left == right


def forward(per_block, q_ref, k_ref, v_ref, probs_ref, total):
    rows, width = q_ref.shape
    scaling = 1.0 / math.sqrt(HEAD_DIM)
    keep = None if per_block is None else same_patch(rows, per_block)
    total[...] = jnp.zeros_like(total)
    for head, (start, size, offset) in enumerate(windows(width)):
        lanes = slice(start, start + size)
        logits = dot(head_only(q_ref[:, lanes], offset), k_ref[:, lanes], NT) * scaling
        if keep is not None:
            logits = jnp.where(keep, logits, -1e30)
        lifted = jnp.exp(logits - jnp.max(logits, axis=-1, keepdims=True))
        probs = lifted * (1.0 / jnp.sum(lifted, axis=-1, keepdims=True))
        probs_ref[head] = probs
        total[:, lanes] += dot(probs.astype(BF16), head_only(v_ref[:, lanes], offset), NN)


def backward(q_ref, k_ref, v_ref, g_ref, probs_ref, dq_sum, dk_sum, dv_sum):
    dq_sum[...] = jnp.zeros_like(dq_sum)
    dk_sum[...] = jnp.zeros_like(dk_sum)
    dv_sum[...] = jnp.zeros_like(dv_sum)
    for head, (start, size, offset) in enumerate(windows(q_ref.shape[1])):
        lanes = slice(start, start + size)
        probs = probs_ref[head]
        step = head_only(g_ref[:, lanes], offset)
        upstream = dot(step, v_ref[:, lanes], NT)
        dv_sum[:, lanes] += dot(probs.astype(BF16), step, TN)
        mean = jnp.sum(probs * upstream, axis=-1, keepdims=True)
        dscore = (probs * (upstream - mean)).astype(BF16)
        dq_sum[:, lanes] += dot(dscore, head_only(k_ref[:, lanes], offset), NN)
        dk_sum[:, lanes] += dot(dscore, head_only(q_ref[:, lanes], offset), TN)


def space_forward_kernel(q_ref, k_ref, v_ref, out_ref, probs_ref, total):
    forward(None, q_ref, k_ref, v_ref, probs_ref, total)
    out_ref[...] = total[...].astype(BF16)


def space_backward_kernel(q_ref, k_ref, v_ref, g_ref, probs_ref, dq_ref, dk_ref, dv_ref, *sums):
    scaling = 1.0 / math.sqrt(HEAD_DIM)
    backward(q_ref, k_ref, v_ref, g_ref, probs_ref, *sums)
    dq_ref[...] = (sums[0][...] * scaling).astype(BF16)
    dk_ref[...] = (sums[1][...] * scaling).astype(BF16)
    dv_ref[...] = sums[2][...].astype(BF16)


def pack_kernel(count, where_ref, *refs):
    groups = refs[0].shape[0]
    refs, (weight_ref, low_ref, high_ref) = refs[:count] + refs[count + 1 : -2], (refs[count],) + refs[-2:]
    low_ref[...] = weight_ref[:1]
    high_ref[...] = weight_ref[1:]
    for i in range(groups):
        for j in range(count):
            refs[count + i][j] = refs[j][where_ref[1] ^ i]


def unpack_kernel(where_ref, *refs):
    count = refs[0].shape[0]
    groups = len(refs) - count
    for i in range(groups):
        for j in range(count):
            refs[groups + j][where_ref[1] ^ i] = refs[i][j]


def time_forward_kernel(groups, *refs):
    pieces, outs = refs[:groups], refs[groups : 2 * groups]
    probs_ref, qkv_ref, total = refs[2 * groups :]
    per_block = pieces[0].shape[1]
    for i in range(groups):
        qkv_ref[:, per_block * i : per_block * (i + 1), :] = pieces[i][...]
    forward(per_block, qkv_ref.at[0], qkv_ref.at[1], qkv_ref.at[2], probs_ref, total)
    for i in range(groups):
        outs[i][...] = total[per_block * i : per_block * (i + 1), :].astype(BF16)


def time_backward_kernel(groups, *refs):
    pieces, (qkv_ref, probs_ref) = refs[:groups], refs[groups : groups + 2]
    outs = refs[groups + 2 : 2 * groups + 2]
    step, *sums = refs[2 * groups + 2 :]
    per_block = pieces[0].shape[0]
    for i in range(groups):
        step[per_block * i : per_block * (i + 1), :] = pieces[i][...]
    backward(qkv_ref.at[0], qkv_ref.at[1], qkv_ref.at[2], step, probs_ref, *sums)
    scaling = 1.0 / math.sqrt(HEAD_DIM)
    for i in range(groups):
        rows = slice(per_block * i, per_block * (i + 1))
        outs[i][0] = (sums[0][rows, :] * scaling).astype(BF16)
        outs[i][1] = (sums[1][rows, :] * scaling).astype(BF16)
        outs[i][2] = sums[2][rows, :].astype(BF16)


def project_kernel(groups, where_ref, *refs):
    pieces, (space_ref, target_ref, weight_ref) = refs[:groups], refs[groups : groups + 3]
    pair_ref, home_ref = refs[groups + 3 : groups + 5]
    outs, total = refs[groups + 5 : 2 * groups + 5], refs[2 * groups + 5]
    per_block = pieces[0].shape[0]
    for i in range(groups):
        rows = slice(per_block * i, per_block * (i + 1))
        total[rows, :] = space_ref[where_ref[1] ^ i].astype(F32) + pieces[i][...].astype(F32)
    comb = total[...].astype(BF16)
    pair_ref[0] = comb
    for i in range(groups):
        rows = slice(per_block * i, per_block * (i + 1))
        total[rows, :] = target_ref[where_ref[1] ^ i].astype(F32)
    og = (dot(comb, weight_ref[...], NN) - total[...]).astype(BF16)
    pair_ref[1] = og
    total[...] = dot(og, weight_ref[...], NT)
    for i in range(groups):
        piece = total[per_block * i : per_block * (i + 1), :].astype(BF16)
        outs[i][...] = piece
        home_ref[where_ref[1] ^ i] = piece


def stack_kernel(*refs):
    for i, ref in enumerate(refs[:-1]):
        size = ref.shape[0]
        refs[-1][i * size : (i + 1) * size] = ref[...]


def weight_kernel(orders, where_ref, *refs):
    for i, ref in enumerate(refs[:-1]):
        half, other = i // 2, i % 2
        for j, bits in enumerate(orders[half]):
            refs[-1][where_ref[0] ^ (2 * bits + other), half] = ref[j]


def halve_kernel(keep_ref, came_ref, *outs):
    total = keep_ref[...] + came_ref[...].astype(F32)
    half = total.shape[0] // 2
    if half == 0:
        outs[0][...] = total.astype(outs[0].dtype)
    else:
        outs[0][...] = total[:half]
        outs[1][...] = total[half:].astype(BF16)


def turn_kernel(order, where_ref, *refs):
    *ins, keep_ref, send_ref, total = refs
    at = 0
    for keep, came in zip(ins[::2], ins[1::2]):
        rows = keep.shape[1]
        total[at : at + rows] = keep[0] + came[0].astype(F32)
        at += rows
    half = len(order) // 2
    for i, bits in enumerate(order):
        piece = total[where_ref[1] ^ bits]
        if i < half:
            keep_ref[i] = piece
        else:
            send_ref[i - half] = piece.astype(BF16)


def join_kernel(scaling, order, where_ref, mine_ref, other_ref, out_ref):
    size, width = mine_ref.shape[-1], out_ref.shape[-1]
    first = (where_ref[0] & 1) == 0
    for i, bits in enumerate(order):
        mine, other = mine_ref[i].astype(F32) * scaling, other_ref[i].astype(F32) * scaling
        chip = (where_ref[0] >> 1) ^ bits
        out_ref[chip, :, :size] = jnp.where(first, mine, other)
        out_ref[chip, :, size:] = jnp.where(first, other, mine)[:, 2 * size - width :]


def grad_kernel(orders, where_ref, mine_ref, other_ref, *refs):
    outs, total = refs[:-1], refs[-1]
    half, _, size = outs[0].shape[1:]
    first = pl.multiple_of((where_ref[0] & 1) * (mine_ref.shape[-1] - size), LANES)
    term = dot(mine_ref[0], mine_ref[1, :, pl.ds(first, size)], TN)
    term += dot(other_ref[0], other_ref[1, :, pl.ds(first, size)], TN)
    total[...] = term.reshape(total.shape)
    for i, order in enumerate(orders):
        keep_ref, send_ref = outs[2 * i : 2 * i + 2]
        stays = len(order) // 2
        for j, bits in enumerate(order):
            piece = total[half * i : half * (i + 1), (where_ref[0] >> 1) ^ bits]
            if j < stays:
                keep_ref[j] = piece
            else:
                send_ref[j - stays] = piece.astype(BF16)


def call(body, outs, scratch, where, *args, cost=COST):
    in_specs = [pl.BlockSpec(memory_space=pltpu.VMEM)] * len(args)
    if where is not None:
        in_specs = [pl.BlockSpec(memory_space=pltpu.SMEM)] + in_specs
        args = (where,) + args
    return pl.pallas_call(
        body,
        out_shape=tuple(jax.ShapeDtypeStruct(*out) for out in outs),
        in_specs=in_specs,
        out_specs=(pl.BlockSpec(memory_space=pltpu.VMEM),) * len(outs),
        scratch_shapes=[pltpu.VMEM(*item) for item in scratch],
        cost_estimate=pl.CostEstimate(flops=cost, bytes_accessed=10, transcendentals=0),
        compiler_params=pltpu.CompilerParams(vmem_limit_bytes=VMEM_BYTES),
    )(*args)


def swap(array, axis, bits):
    size = lax.axis_size(axis)
    return lax.ppermute(array, axis, [(i, i ^ bits) for i in range(size)])


def after(value, *others):
    return lax.optimization_barrier((value,) + others)[0]


def stack(left, right):
    shape = (2 * left.shape[0],) + left.shape[1:]
    return call(stack_kernel, [(shape, BF16)], [], None, left, right)[0]


def doubled(held, bits):
    order = [0]
    for bit in bits:
        held = stack(held, swap(held, "dp", 2 * bit))
        order += [item ^ bit for item in order]
    return held, order


def gather_weight(halves, where):
    size = lax.axis_size("dp")
    bits = bits_of(size // 2)
    low, low_order = doubled(halves[0], bits)
    high, high_order = doubled(halves[1], bits[::-1])
    _, rows, width = low.shape
    (full,) = call(
        functools.partial(weight_kernel, [low_order, high_order]),
        [((size, 2, rows, width), BF16)],
        [],
        where,
        low,
        swap(low, "dp", 1),
        high,
        swap(high, "dp", 1),
    )
    return full.reshape(2 * size * rows, width)


def bits_of(size):
    return [1 << i for i in range(size.bit_length() - 1)]


def halving(bits):
    order = [0]
    for bit in reversed(bits):
        order = order + [item ^ bit for item in order]
    return order


def halved(keep, came):
    count, rest = keep.shape[0], keep.shape[1:]
    if count == 1:
        return call(halve_kernel, [(keep.shape, BF16)], [], None, keep, came, cost=SMALL)
    half = (count // 2,) + rest
    return call(halve_kernel, [(half, F32), (half, BF16)], [], None, keep, came, cost=SMALL)


def weight_gradient(pair, earlier, scaling, where):
    width = pair.shape[-1]
    chip_size, groups = lax.axis_size("dp") // 2, lax.axis_size("seq")
    rows = width // groups // chip_size
    size = -(-width // (2 * LANES)) * LANES
    bits, seq_bits = bits_of(chip_size), bits_of(groups)
    ways = [bits, bits[::-1]]
    cut = (chip_size // 2, groups // 2, rows, size)
    terms = call(
        functools.partial(grad_kernel, [halving(way) for way in ways]),
        [(cut, F32), (cut, BF16)] * 2,
        [((groups, chip_size, rows, size), F32)],
        where,
        pair,
        swap(pair, "dp", 1),
    )
    state = [[terms[0], swap(terms[1], "dp", 2 * ways[0][0])]]
    state += [[terms[2], swap(terms[3], "dp", 2 * ways[1][0])]]
    state[0][0] = after(state[0][0], earlier)
    for i in range(1, len(bits)):
        for j in range(2):
            keep, send = halved(*state[j])
            state[j] = [keep, swap(send, "dp", 2 * ways[j][i])]
    order = halving(seq_bits)
    cut = (groups // 2, rows, size)
    keep, send = call(
        functools.partial(turn_kernel, order),
        [(cut, F32), (cut, BF16)],
        [((groups, rows, size), F32)],
        where,
        *state[0],
        *state[1],
        cost=SMALL,
    )
    for bit in seq_bits[:-1]:
        keep, send = halved(keep, swap(send, "seq", bit))
    (total,) = halved(keep, swap(send, "seq", seq_bits[-1]))
    mine, order = doubled(total, bits)
    (whole,) = call(
        functools.partial(join_kernel, scaling, order),
        [((chip_size, rows, width), F32)],
        [],
        where,
        mine,
        swap(mine, "dp", 1),
        cost=SMALL,
    )
    return whole.reshape(chip_size * rows, width)


def divides(width):
    cuts = lax.axis_size("seq") * lax.axis_size("dp") // 2
    return width % (cuts * 8) == 0


def shards(q_space, k_space, v_space, q_time, k_time, v_time, weight, target):
    groups = lax.axis_size("seq")
    where = jnp.stack([lax.axis_index("dp"), lax.axis_index("seq")])
    rows, width = q_space.shape[1:]
    heads = width // HEAD_DIM
    per_block = rows // groups
    blocks, piece, full = (groups, per_block, width), (per_block, width), (rows, width)

    def exchange(pieces):
        return list(pieces[:1]) + [swap(pieces[i], "seq", i) for i in range(1, groups)]

    half = (1, weight.shape[0] // 2, width)
    *sent, low, high = call(
        functools.partial(pack_kernel, 3),
        [((3,) + piece, BF16)] * groups + [(half, BF16)] * 2,
        [],
        where,
        *[item.reshape(blocks) for item in (q_time, k_time, v_time)],
        weight.reshape((2,) + half[1:]),
    )
    there = exchange(sent)
    full_weight = gather_weight((low, high), where)
    space = [item.reshape(full) for item in (q_space, k_space, v_space)]
    out_space, probs_s = call(
        space_forward_kernel,
        [(full, BF16), ((heads, rows, rows), F32)],
        [(full, F32)],
        None,
        *space,
    )
    there[0] = after(there[0], out_space, full_weight)
    *out_time, probs_t, time_qkv = call(
        functools.partial(time_forward_kernel, groups),
        [(piece, BF16)] * groups + [((heads, rows, rows), F32), ((3,) + full, BF16)],
        [(full, F32)],
        None,
        *there,
    )
    pair, step_home, *steps = call(
        functools.partial(project_kernel, groups),
        [((2,) + full, BF16), (blocks, BF16)] + [(piece, BF16)] * groups,
        [(full, F32)],
        where,
        *exchange(out_time),
        out_space.reshape(blocks),
        target.reshape(blocks),
        full_weight,
    )
    scaling = 1.0 / math.sqrt(lax.axis_size("dp") * groups * rows)
    steps = exchange(steps)
    time_grads = call(
        functools.partial(time_backward_kernel, groups),
        [((3,) + piece, BF16)] * groups,
        [(full, BF16)] + [(full, F32)] * 3,
        None,
        *steps,
        time_qkv,
        probs_t,
    )
    if divides(width):
        weight_grad = weight_gradient(pair, time_grads[0], scaling, where)
    else:
        term = dot(pair[0], pair[1], TN).astype(BF16)
        share = lax.psum_scatter(term, "seq", scatter_dimension=0, tiled=True)
        weight_grad = lax.psum(share, "dp").astype(F32) * scaling
    space_grads = call(
        space_backward_kernel,
        [(full, BF16)] * 3,
        [(full, F32)] * 3,
        None,
        *space,
        after(step_home, time_grads[0]).reshape(full),
        probs_s,
    )
    back = exchange(time_grads)
    back[0] = after(back[0], weight_grad)
    back = call(unpack_kernel, [(blocks, BF16)] * 3, [], where, *back)
    outs = [item.reshape(q_space.shape) for item in list(space_grads) + list(back)]
    return tuple(outs) + (weight_grad,)


def solution(mesh):
    tokens = P("dp", "seq", None)
    return jax.shard_map(
        shards,
        mesh=mesh,
        in_specs=(tokens,) * 6 + (P("dp", None), tokens),
        out_specs=(tokens,) * 6 + (P("seq", None),),
        check_vma=False,
    )
```

```python
import functools
import math

import jax
import jax.numpy as jnp
from jax import lax
from jax.experimental import pallas as pl
from jax.experimental.pallas import tpu as pltpu
from jax.sharding import PartitionSpec as P

HEAD_DIM = 72
LANES = 128
VMEM_BYTES = 24 * 1024 * 1024
COST = 10**10
SMALL = 10
F32 = jnp.float32
BF16 = jnp.bfloat16
NT = (((1,), (1,)), ((), ()))
NN = (((1,), (0,)), ((), ()))
TN = (((0,), (0,)), ((), ()))


def dot(left, right, form):
    return lax.dot_general(left, right, form, preferred_element_type=F32)


def windows(width):
    found = []
    for head in range(width // HEAD_DIM):
        first = head * HEAD_DIM
        start = first // LANES * LANES
        size = -(-(first + HEAD_DIM - start) // LANES) * LANES
        found.append((start, size, first - start))
    return found


def head_only(block, offset):
    lane = lax.broadcasted_iota(jnp.int32, (1, block.shape[1]), 1)
    inside = (lane >= offset) & (lane < offset + HEAD_DIM)
    return jnp.where(inside, block, jnp.zeros_like(block))


def same_patch(rows, per_block):
    left = lax.broadcasted_iota(jnp.int32, (rows, 1), 0) % per_block
    right = lax.broadcasted_iota(jnp.int32, (1, rows), 1) % per_block
    return left == right


def forward(per_block, q_ref, k_ref, v_ref, probs_ref, total):
    rows, width = q_ref.shape
    scaling = 1.0 / math.sqrt(HEAD_DIM)
    keep = None if per_block is None else same_patch(rows, per_block)
    total[...] = jnp.zeros_like(total)
    for head, (start, size, offset) in enumerate(windows(width)):
        lanes = slice(start, start + size)
        logits = dot(head_only(q_ref[:, lanes], offset), k_ref[:, lanes], NT) * scaling
        if keep is not None:
            logits = jnp.where(keep, logits, -1e30)
        lifted = jnp.exp(logits - jnp.max(logits, axis=-1, keepdims=True))
        probs = lifted * (1.0 / jnp.sum(lifted, axis=-1, keepdims=True))
        probs_ref[head] = probs
        total[:, lanes] += dot(probs.astype(BF16), head_only(v_ref[:, lanes], offset), NN)


def backward(q_ref, k_ref, v_ref, g_ref, probs_ref, dq_sum, dk_sum, dv_sum):
    dq_sum[...] = jnp.zeros_like(dq_sum)
    dk_sum[...] = jnp.zeros_like(dk_sum)
    dv_sum[...] = jnp.zeros_like(dv_sum)
    for head, (start, size, offset) in enumerate(windows(q_ref.shape[1])):
        lanes = slice(start, start + size)
        probs = probs_ref[head]
        step = head_only(g_ref[:, lanes], offset)
        upstream = dot(step, v_ref[:, lanes], NT)
        dv_sum[:, lanes] += dot(probs.astype(BF16), step, TN)
        mean = jnp.sum(probs * upstream, axis=-1, keepdims=True)
        dscore = (probs * (upstream - mean)).astype(BF16)
        dq_sum[:, lanes] += dot(dscore, head_only(k_ref[:, lanes], offset), NN)
        dk_sum[:, lanes] += dot(dscore, head_only(q_ref[:, lanes], offset), TN)


def space_forward_kernel(q_ref, k_ref, v_ref, out_ref, probs_ref, total):
    forward(None, q_ref, k_ref, v_ref, probs_ref, total)
    out_ref[...] = total[...].astype(BF16)


def space_backward_kernel(q_ref, k_ref, v_ref, g_ref, probs_ref, dq_ref, dk_ref, dv_ref, *sums):
    scaling = 1.0 / math.sqrt(HEAD_DIM)
    backward(q_ref, k_ref, v_ref, g_ref, probs_ref, *sums)
    dq_ref[...] = (sums[0][...] * scaling).astype(BF16)
    dk_ref[...] = (sums[1][...] * scaling).astype(BF16)
    dv_ref[...] = sums[2][...].astype(BF16)


def pack_kernel(first, where_ref, *refs):
    count = refs[-1].shape[0]
    for i, piece_ref in enumerate(refs[count:]):
        for j, array_ref in enumerate(refs[:count]):
            piece_ref[j] = array_ref[where_ref[1] ^ (first + i)]


def halves_kernel(weight_ref, low_ref, high_ref):
    low_ref[...] = weight_ref[:1]
    high_ref[...] = weight_ref[1:]


def unpack_kernel(where_ref, *refs):
    count = refs[0].shape[0]
    groups = len(refs) - count
    for i in range(groups):
        for j in range(count):
            refs[groups + j][where_ref[1] ^ i] = refs[i][j]


def time_forward_kernel(groups, *refs):
    pieces, outs = refs[:groups], refs[groups : 2 * groups]
    probs_ref, qkv_ref, total = refs[2 * groups :]
    per_block = pieces[0].shape[1]
    for i in range(groups):
        qkv_ref[:, per_block * i : per_block * (i + 1), :] = pieces[i][...]
    forward(per_block, qkv_ref.at[0], qkv_ref.at[1], qkv_ref.at[2], probs_ref, total)
    for i in range(groups):
        outs[i][...] = total[per_block * i : per_block * (i + 1), :].astype(BF16)


def time_backward_kernel(groups, *refs):
    pieces, (qkv_ref, probs_ref) = refs[:groups], refs[groups : groups + 2]
    outs = refs[groups + 2 : 2 * groups + 2]
    step, *sums = refs[2 * groups + 2 :]
    per_block = pieces[0].shape[0]
    for i in range(groups):
        step[per_block * i : per_block * (i + 1), :] = pieces[i][...]
    backward(qkv_ref.at[0], qkv_ref.at[1], qkv_ref.at[2], step, probs_ref, *sums)
    scaling = 1.0 / math.sqrt(HEAD_DIM)
    for i in range(groups):
        rows = slice(per_block * i, per_block * (i + 1))
        outs[i][0] = (sums[0][rows, :] * scaling).astype(BF16)
        outs[i][1] = (sums[1][rows, :] * scaling).astype(BF16)
        outs[i][2] = sums[2][rows, :].astype(BF16)


def project_kernel(groups, where_ref, *refs):
    pieces, (space_ref, target_ref, weight_ref) = refs[:groups], refs[groups : groups + 3]
    pair_ref, home_ref = refs[groups + 3 : groups + 5]
    outs, total = refs[groups + 5 : 2 * groups + 5], refs[2 * groups + 5]
    per_block = pieces[0].shape[0]
    for i in range(groups):
        rows = slice(per_block * i, per_block * (i + 1))
        total[rows, :] = space_ref[where_ref[1] ^ i].astype(F32) + pieces[i][...].astype(F32)
    comb = total[...].astype(BF16)
    pair_ref[0] = comb
    for i in range(groups):
        rows = slice(per_block * i, per_block * (i + 1))
        total[rows, :] = target_ref[where_ref[1] ^ i].astype(F32)
    og = (dot(comb, weight_ref[...], NN) - total[...]).astype(BF16)
    pair_ref[1] = og
    total[...] = dot(og, weight_ref[...], NT)
    for i in range(groups):
        piece = total[per_block * i : per_block * (i + 1), :].astype(BF16)
        outs[i][...] = piece
        home_ref[where_ref[1] ^ i] = piece


def stack_kernel(*refs):
    for i, ref in enumerate(refs[:-1]):
        size = ref.shape[0]
        refs[-1][i * size : (i + 1) * size] = ref[...]


def weight_kernel(orders, where_ref, *refs):
    for i, ref in enumerate(refs[:-1]):
        half, other = i // 2, i % 2
        for j, bits in enumerate(orders[half]):
            refs[-1][where_ref[0] ^ (2 * bits + other), half] = ref[j]


def halve_kernel(keep_ref, came_ref, *outs):
    total = keep_ref[...] + came_ref[...].astype(F32)
    half = total.shape[0] // 2
    if half == 0:
        outs[0][...] = total.astype(outs[0].dtype)
    else:
        outs[0][...] = total[:half]
        outs[1][...] = total[half:].astype(BF16)


def turn_kernel(order, where_ref, *refs):
    *ins, keep_ref, send_ref, total = refs
    at = 0
    for keep, came in zip(ins[::2], ins[1::2]):
        rows = keep.shape[1]
        total[at : at + rows] = keep[0] + came[0].astype(F32)
        at += rows
    half = len(order) // 2
    for i, bits in enumerate(order):
        piece = total[where_ref[1] ^ bits]
        if i < half:
            keep_ref[i] = piece
        else:
            send_ref[i - half] = piece.astype(BF16)


def join_kernel(scaling, order, where_ref, mine_ref, other_ref, out_ref):
    size, width = mine_ref.shape[-1], out_ref.shape[-1]
    first = (where_ref[0] & 1) == 0
    for i, bits in enumerate(order):
        mine, other = mine_ref[i].astype(F32) * scaling, other_ref[i].astype(F32) * scaling
        chip = (where_ref[0] >> 1) ^ bits
        out_ref[chip, :, :size] = jnp.where(first, mine, other)
        out_ref[chip, :, size:] = jnp.where(first, other, mine)[:, 2 * size - width :]


def grad_kernel(orders, where_ref, mine_ref, other_ref, *refs):
    outs, total = refs[:-1], refs[-1]
    half, _, size = outs[0].shape[1:]
    first = pl.multiple_of((where_ref[0] & 1) * (mine_ref.shape[-1] - size), LANES)
    term = dot(mine_ref[0], mine_ref[1, :, pl.ds(first, size)], TN)
    term += dot(other_ref[0], other_ref[1, :, pl.ds(first, size)], TN)
    total[...] = term.reshape(total.shape)
    for i, order in enumerate(orders):
        keep_ref, send_ref = outs[2 * i : 2 * i + 2]
        stays = len(order) // 2
        for j, bits in enumerate(order):
            piece = total[half * i : half * (i + 1), (where_ref[0] >> 1) ^ bits]
            if j < stays:
                keep_ref[j] = piece
            else:
                send_ref[j - stays] = piece.astype(BF16)


def call(body, outs, scratch, where, *args, cost=COST):
    in_specs = [pl.BlockSpec(memory_space=pltpu.VMEM)] * len(args)
    if where is not None:
        in_specs = [pl.BlockSpec(memory_space=pltpu.SMEM)] + in_specs
        args = (where,) + args
    return pl.pallas_call(
        body,
        out_shape=tuple(jax.ShapeDtypeStruct(*out) for out in outs),
        in_specs=in_specs,
        out_specs=(pl.BlockSpec(memory_space=pltpu.VMEM),) * len(outs),
        scratch_shapes=[pltpu.VMEM(*item) for item in scratch],
        cost_estimate=pl.CostEstimate(flops=cost, bytes_accessed=10, transcendentals=0),
        compiler_params=pltpu.CompilerParams(vmem_limit_bytes=VMEM_BYTES),
    )(*args)


def swap(array, axis, bits):
    size = lax.axis_size(axis)
    return lax.ppermute(array, axis, [(i, i ^ bits) for i in range(size)])


def after(value, *others):
    return lax.optimization_barrier((value,) + others)[0]


def stack(left, right, cost=COST):
    shape = (2 * left.shape[0],) + left.shape[1:]
    return call(stack_kernel, [(shape, BF16)], [], None, left, right, cost=cost)[0]


def doubled(held, bits, earlier, last=False):
    order = [0]
    for bit in bits:
        came = swap(held, "dp", 2 * bit)
        if bit == bits[-1 if last else 0] and not last:
            held = after(held, earlier)
        held = stack(held, came, SMALL if last else COST)
        order += [item ^ bit for item in order]
    return held, order


def gather_weight(halves, earlier, where):
    size = lax.axis_size("dp")
    bits = bits_of(size // 2)
    low, low_order = doubled(halves[0], bits, earlier)
    high, high_order = doubled(halves[1], bits[::-1], earlier)
    _, rows, width = low.shape
    (full,) = call(
        functools.partial(weight_kernel, [low_order, high_order]),
        [((size, 2, rows, width), BF16)],
        [],
        where,
        low,
        swap(low, "dp", 1),
        high,
        swap(high, "dp", 1),
    )
    return full.reshape(2 * size * rows, width)


def bits_of(size):
    return [1 << i for i in range(size.bit_length() - 1)]


def halving(bits):
    order = [0]
    for bit in reversed(bits):
        order = order + [item ^ bit for item in order]
    return order


def halved(keep, came):
    count, rest = keep.shape[0], keep.shape[1:]
    if count == 1:
        return call(halve_kernel, [(keep.shape, BF16)], [], None, keep, came, cost=SMALL)
    half = (count // 2,) + rest
    return call(halve_kernel, [(half, F32), (half, BF16)], [], None, keep, came, cost=SMALL)


def weight_gradient(pair, earlier, beside, back, scaling, where):
    width = pair.shape[-1]
    chip_size, groups = lax.axis_size("dp") // 2, lax.axis_size("seq")
    rows = width // groups // chip_size
    size = -(-width // (2 * LANES)) * LANES
    bits, seq_bits = bits_of(chip_size), bits_of(groups)
    ways = [bits, bits[::-1]]
    cut = (chip_size // 2, groups // 2, rows, size)
    terms = call(
        functools.partial(grad_kernel, [halving(way) for way in ways]),
        [(cut, F32), (cut, BF16)] * 2,
        [((groups, chip_size, rows, size), F32)],
        where,
        pair,
        swap(pair, "dp", 1),
    )
    state = [[terms[0], swap(terms[1], "dp", 2 * ways[0][0])]]
    state += [[terms[2], swap(terms[3], "dp", 2 * ways[1][0])]]
    state[0][0] = after(state[0][0], earlier)
    for i in range(1, len(bits)):
        for j in range(2):
            keep, send = halved(*state[j])
            state[j] = [keep, swap(send, "dp", 2 * ways[j][i])]
    order = halving(seq_bits)
    cut = (groups // 2, rows, size)
    keep, send = call(
        functools.partial(turn_kernel, order),
        [(cut, F32), (cut, BF16)],
        [((groups, rows, size), F32)],
        where,
        *state[0],
        *state[1],
        cost=SMALL,
    )
    keep = after(keep, beside)
    for bit in seq_bits[:-1]:
        keep, send = halved(keep, swap(send, "seq", bit))
    keep = after(keep, back[-1])
    (total,) = halved(keep, swap(send, "seq", seq_bits[-1]))
    mine, order = doubled(total, bits, back[len(back) // 2], last=True)
    (whole,) = call(
        functools.partial(join_kernel, scaling, order),
        [((chip_size, rows, width), F32)],
        [],
        where,
        mine,
        swap(mine, "dp", 1),
        cost=SMALL,
    )
    return whole.reshape(chip_size * rows, width)


def divides(width):
    cuts = lax.axis_size("seq") * lax.axis_size("dp") // 2
    return width % (cuts * 8) == 0


def shards(q_space, k_space, v_space, q_time, k_time, v_time, weight, target):
    groups = lax.axis_size("seq")
    where = jnp.stack([lax.axis_index("dp"), lax.axis_index("seq")])
    rows, width = q_space.shape[1:]
    heads = width // HEAD_DIM
    per_block = rows // groups
    blocks, piece, full = (groups, per_block, width), (per_block, width), (rows, width)

    def exchange(pieces):
        return list(pieces[:1]) + [swap(pieces[i], "seq", i) for i in range(1, groups)]

    times = [item.reshape(blocks) for item in (q_time, k_time, v_time)]
    sent = call(
        functools.partial(pack_kernel, 1),
        [((3,) + piece, BF16)] * (groups - 1),
        [],
        where,
        *times,
        cost=SMALL,
    )
    (own,) = call(
        functools.partial(pack_kernel, 0),
        [((3,) + piece, BF16)],
        [],
        after(where, sent[0]),
        *times,
    )
    half = (1, weight.shape[0] // 2, width)
    halves = call(
        halves_kernel, [(half, BF16)] * 2, [], None, after(weight, sent[0]).reshape((2,) + half[1:])
    )
    there = exchange([own, *sent])
    full_weight = gather_weight(halves, own, where)
    space = [item.reshape(full) for item in (q_space, k_space, v_space)]
    out_space, probs_s = call(
        space_forward_kernel,
        [(full, BF16), ((heads, rows, rows), F32)],
        [(full, F32)],
        None,
        *space,
    )
    there[0] = after(there[0], out_space)
    *out_time, probs_t, time_qkv = call(
        functools.partial(time_forward_kernel, groups),
        [(piece, BF16)] * groups + [((heads, rows, rows), F32), ((3,) + full, BF16)],
        [(full, F32)],
        None,
        *there,
    )
    pair, step_home, *steps = call(
        functools.partial(project_kernel, groups),
        [((2,) + full, BF16), (blocks, BF16)] + [(piece, BF16)] * groups,
        [(full, F32)],
        where,
        *exchange(out_time),
        out_space.reshape(blocks),
        target.reshape(blocks),
        full_weight,
    )
    scaling = 1.0 / math.sqrt(lax.axis_size("dp") * groups * rows)
    steps = exchange(steps)
    time_grads = call(
        functools.partial(time_backward_kernel, groups),
        [((3,) + piece, BF16)] * groups,
        [(full, BF16)] + [(full, F32)] * 3,
        None,
        *steps,
        time_qkv,
        probs_t,
    )
    space_grads = call(
        space_backward_kernel,
        [(full, BF16)] * 3,
        [(full, F32)] * 3,
        None,
        *space,
        after(step_home, time_grads[0]).reshape(full),
        probs_s,
    )
    back = exchange(time_grads)
    if divides(width):
        weight_grad = weight_gradient(pair, time_grads[0], space_grads[0], back, scaling, where)
    else:
        term = dot(pair[0], pair[1], TN).astype(BF16)
        share = lax.psum_scatter(term, "seq", scatter_dimension=0, tiled=True)
        weight_grad = lax.psum(share, "dp").astype(F32) * scaling
    back = call(unpack_kernel, [(blocks, BF16)] * 3, [], where, *back)
    outs = [item.reshape(q_space.shape) for item in list(space_grads) + list(back)]
    return tuple(outs) + (weight_grad,)


def solution(mesh):
    tokens = P("dp", "seq", None)
    return jax.shard_map(
        shards,
        mesh=mesh,
        in_specs=(tokens,) * 6 + (P("dp", None), tokens),
        out_specs=(tokens,) * 6 + (P("seq", None),),
        check_vma=False,
    )
```

```python
import functools
import math

import jax
import jax.numpy as jnp
from jax import lax
from jax.experimental import pallas as pl
from jax.experimental.pallas import tpu as pltpu
from jax.sharding import PartitionSpec as P

HEAD_DIM = 72
LANES = 128
VMEM_BYTES = 24 * 1024 * 1024
COST = 2 * 10**10
SMALL = 10
F32 = jnp.float32
BF16 = jnp.bfloat16
NT = (((1,), (1,)), ((), ()))
NN = (((1,), (0,)), ((), ()))
TN = (((0,), (0,)), ((), ()))


def dot(left, right, form):
    return lax.dot_general(left, right, form, preferred_element_type=F32)


def windows(width):
    found = []
    for head in range(width // HEAD_DIM):
        first = head * HEAD_DIM
        start = first // LANES * LANES
        size = -(-(first + HEAD_DIM - start) // LANES) * LANES
        found.append((start, size, first - start))
    return found


def head_only(block, offset):
    lane = lax.broadcasted_iota(jnp.int32, (1, block.shape[1]), 1)
    inside = (lane >= offset) & (lane < offset + HEAD_DIM)
    return jnp.where(inside, block, jnp.zeros_like(block))


def reverse(number, size):
    found = 0
    for i in range(size.bit_length() - 1):
        found = 2 * found + (number >> i & 1)
    return found


def by_core(core, even, odd):
    return even + core * (odd - even)


def same_patch(rows, per_block):
    left = lax.broadcasted_iota(jnp.int32, (rows, 1), 0) % per_block
    right = lax.broadcasted_iota(jnp.int32, (1, rows), 1) % per_block
    return left == right


def forward(per_block, q_ref, k_ref, v_ref, probs_ref, total):
    rows, width = q_ref.shape
    scaling = 1.0 / math.sqrt(HEAD_DIM)
    keep = None if per_block is None else same_patch(rows, per_block)
    total[...] = jnp.zeros_like(total)
    for head, (start, size, offset) in enumerate(windows(width)):
        lanes = slice(start, start + size)
        logits = dot(head_only(q_ref[:, lanes], offset), k_ref[:, lanes], NT) * scaling
        if keep is not None:
            logits = jnp.where(keep, logits, -1e30)
        lifted = jnp.exp(logits - jnp.max(logits, axis=-1, keepdims=True))
        probs = lifted * (1.0 / jnp.sum(lifted, axis=-1, keepdims=True))
        probs_ref[head] = probs
        total[:, lanes] += dot(probs.astype(BF16), head_only(v_ref[:, lanes], offset), NN)


def backward(q_ref, k_ref, v_ref, g_ref, probs_ref, dq_sum, dk_sum, dv_sum):
    dq_sum[...] = jnp.zeros_like(dq_sum)
    dk_sum[...] = jnp.zeros_like(dk_sum)
    dv_sum[...] = jnp.zeros_like(dv_sum)
    for head, (start, size, offset) in enumerate(windows(q_ref.shape[1])):
        lanes = slice(start, start + size)
        probs = probs_ref[head]
        step = head_only(g_ref[:, lanes], offset)
        upstream = dot(step, v_ref[:, lanes], NT)
        dv_sum[:, lanes] += dot(probs.astype(BF16), step, TN)
        mean = jnp.sum(probs * upstream, axis=-1, keepdims=True)
        dscore = (probs * (upstream - mean)).astype(BF16)
        dq_sum[:, lanes] += dot(dscore, head_only(k_ref[:, lanes], offset), NN)
        dk_sum[:, lanes] += dot(dscore, head_only(q_ref[:, lanes], offset), TN)


def space_forward_kernel(q_ref, k_ref, v_ref, out_ref, probs_ref, total):
    forward(None, q_ref, k_ref, v_ref, probs_ref, total)
    out_ref[...] = total[...].astype(BF16)


def space_backward_kernel(q_ref, k_ref, v_ref, g_ref, probs_ref, dq_ref, dk_ref, dv_ref, *sums):
    scaling = 1.0 / math.sqrt(HEAD_DIM)
    backward(q_ref, k_ref, v_ref, g_ref, probs_ref, *sums)
    dq_ref[...] = (sums[0][...] * scaling).astype(BF16)
    dk_ref[...] = (sums[1][...] * scaling).astype(BF16)
    dv_ref[...] = sums[2][...].astype(BF16)


def pack_kernel(first, where_ref, *refs):
    count = refs[-1].shape[0]
    for i, piece_ref in enumerate(refs[count:]):
        for j, array_ref in enumerate(refs[:count]):
            piece_ref[j] = array_ref[where_ref[1] ^ (first + i)]


def unpack_kernel(where_ref, *refs):
    count = refs[0].shape[0]
    groups = len(refs) - count
    for i in range(groups):
        for j in range(count):
            refs[groups + j][where_ref[1] ^ i] = refs[i][j]


def time_forward_kernel(groups, *refs):
    pieces, (probs_ref, qkv_ref, total) = refs[:groups], refs[groups:]
    per_block = pieces[0].shape[1]
    for i in range(groups):
        qkv_ref[:, per_block * i : per_block * (i + 1), :] = pieces[i][...]
    forward(per_block, qkv_ref.at[0], qkv_ref.at[1], qkv_ref.at[2], probs_ref, total)


def time_backward_kernel(groups, step_ref, qkv_ref, probs_ref, *refs):
    outs, sums = refs[:groups], refs[groups:]
    per_block = outs[0].shape[1]
    backward(qkv_ref.at[0], qkv_ref.at[1], qkv_ref.at[2], step_ref, probs_ref, *sums)
    scaling = 1.0 / math.sqrt(HEAD_DIM)
    for i in range(groups):
        rows = slice(per_block * i, per_block * (i + 1))
        outs[i][0] = (sums[0][rows, :] * scaling).astype(BF16)
        outs[i][1] = (sums[1][rows, :] * scaling).astype(BF16)
        outs[i][2] = sums[2][rows, :].astype(BF16)


def project_kernel(groups, *refs):
    pieces, (time_ref, weight_ref) = refs[:groups], refs[groups : groups + 2]
    pair_ref, step_ref = refs[groups + 2 : groups + 4]
    outs, total = refs[groups + 4 : 2 * groups + 4], refs[2 * groups + 4]
    per_block = pieces[0].shape[1]
    for i in range(groups):
        rows = slice(per_block * i, per_block * (i + 1))
        total[rows, :] = pieces[i][0].astype(F32) + time_ref[rows, :]
    comb = total[...].astype(BF16)
    pair_ref[0] = comb
    for i in range(groups):
        total[per_block * i : per_block * (i + 1), :] = pieces[i][1].astype(F32)
    og = (dot(comb, weight_ref[...], NN) - total[...]).astype(BF16)
    pair_ref[1] = og
    total[...] = dot(og, weight_ref[...], NT)
    step_ref[...] = total[...].astype(BF16)
    for i in range(groups):
        outs[i][0] = total[per_block * i : per_block * (i + 1), :].astype(BF16)


def copy_kernel(in_ref, out_ref):
    out_ref[...] = in_ref[...]


def stack_kernel(*refs):
    for i, ref in enumerate(refs[:-1]):
        size = ref.shape[0]
        refs[-1][i * size : (i + 1) * size] = ref[...]


def weight_kernel(where_ref, mine_ref, other_ref, out_ref):
    core, chip = where_ref[0] & 1, where_ref[0] >> 1
    size = mine_ref.shape[0]
    for i in range(size):
        back = reverse(i, size)
        out_ref[2 * (chip ^ by_core(core, i, back)) + core] = mine_ref[i]
        out_ref[2 * (chip ^ by_core(core, back, i)) + 1 - core] = other_ref[i]


def halve_kernel(keep_ref, came_ref, *outs):
    total = keep_ref[...] + came_ref[...].astype(F32)
    half = total.shape[0] // 2
    if half == 0:
        outs[0][...] = total.astype(outs[0].dtype)
    else:
        outs[0][...] = total[:half]
        outs[1][...] = total[half:].astype(BF16)


def turn_kernel(order, where_ref, mine_ref, came_ref, keep_ref, send_ref, total):
    total[...] = mine_ref[0] + came_ref[0].astype(F32)
    half = len(order) // 2
    for i, bits in enumerate(order):
        piece = total[where_ref[1] ^ bits]
        if i < half:
            keep_ref[i] = piece
        else:
            send_ref[i - half] = piece.astype(BF16)


def join_kernel(scaling, where_ref, mine_ref, other_ref, out_ref):
    core, chip = where_ref[0] & 1, where_ref[0] >> 1
    chips, _, size = mine_ref.shape
    first = core == 0
    for i in range(chips):
        back = reverse(i, chips)
        mine = mine_ref[by_core(core, i, back)].astype(F32) * scaling
        other = other_ref[by_core(core, back, i)].astype(F32) * scaling
        out_ref[chip ^ i, :, :size] = jnp.where(first, mine, other)
        out_ref[chip ^ i, :, size:] = jnp.where(first, other, mine)[:, 2 * size - out_ref.shape[-1] :]


def grad_kernel(where_ref, mine_ref, other_ref, keep_ref, send_ref, total):
    core, chip = where_ref[0] & 1, where_ref[0] >> 1
    stays, _, _, size = keep_ref.shape
    first = pl.multiple_of(core * (mine_ref.shape[-1] - size), LANES)
    term = dot(mine_ref[0], mine_ref[1, :, pl.ds(first, size)], TN)
    term += dot(other_ref[0], other_ref[1, :, pl.ds(first, size)], TN)
    total[...] = term.reshape(total.shape)
    for i in range(2 * stays):
        piece = total[:, chip ^ by_core(core, reverse(i, 2 * stays), i)]
        if i < stays:
            keep_ref[i] = piece
        else:
            send_ref[i - stays] = piece.astype(BF16)


def call(body, outs, scratch, where, *args, cost=COST):
    in_specs = [pl.BlockSpec(memory_space=pltpu.VMEM)] * len(args)
    if where is not None:
        in_specs = [pl.BlockSpec(memory_space=pltpu.SMEM)] + in_specs
        args = (where,) + args
    return pl.pallas_call(
        body,
        out_shape=tuple(jax.ShapeDtypeStruct(*out) for out in outs),
        in_specs=in_specs,
        out_specs=(pl.BlockSpec(memory_space=pltpu.VMEM),) * len(outs),
        scratch_shapes=[pltpu.VMEM(*item) for item in scratch],
        cost_estimate=pl.CostEstimate(flops=cost, bytes_accessed=10, transcendentals=0),
        compiler_params=pltpu.CompilerParams(vmem_limit_bytes=VMEM_BYTES),
    )(*args)


def swap(array, axis, bits):
    size = lax.axis_size(axis)
    return lax.ppermute(array, axis, [(i, i ^ bits) for i in range(size)])


def after(value, *others):
    return lax.optimization_barrier((value,) + others)[0]


def stack(left, right, cost=COST):
    shape = (2 * left.shape[0],) + left.shape[1:]
    return call(stack_kernel, [(shape, BF16)], [], None, left, right, cost=cost)[0]


def swap_ways(array, step, count):
    bits = (2 << step, 2 << (count - 1 - step))
    size = lax.axis_size("dp")
    return lax.ppermute(array, "dp", [(i, i ^ bits[i % 2]) for i in range(size)])


def doubled(held, count, *earlier, cost=COST):
    for step in range(count):
        came = swap_ways(held, step, count)
        if step < len(earlier):
            held = after(held, earlier[step])
        held = stack(held, came, cost)
    return held


def gather_weight(weight, earlier, where):
    size = lax.axis_size("dp")
    held = doubled(weight, (size // 2).bit_length() - 1, *earlier)
    (full,) = call(
        weight_kernel,
        [((size,) + weight.shape[1:], BF16)],
        [],
        where,
        held,
        swap(held, "dp", 1),
    )
    return full.reshape(size * weight.shape[1], weight.shape[2])


def bits_of(size):
    return [1 << i for i in range(size.bit_length() - 1)]


def halving(bits):
    order = [0]
    for bit in reversed(bits):
        order = order + [item ^ bit for item in order]
    return order


def halved(keep, came):
    count, rest = keep.shape[0], keep.shape[1:]
    if count == 1:
        return call(halve_kernel, [(keep.shape, BF16)], [], None, keep, came, cost=SMALL)
    half = (count // 2,) + rest
    return call(halve_kernel, [(half, F32), (half, BF16)], [], None, keep, came, cost=SMALL)


def gradient_terms(pair, where):
    width = pair.shape[-1]
    chip_size, groups = lax.axis_size("dp") // 2, lax.axis_size("seq")
    rows = width // groups // chip_size
    size = -(-width // (2 * LANES)) * LANES
    cut = (chip_size // 2, groups, rows, size)
    return call(
        grad_kernel,
        [(cut, F32), (cut, BF16)],
        [((groups, chip_size, rows, size), F32)],
        where,
        pair,
        swap(pair, "dp", 1),
    )


def weight_gradient(terms, width, earlier, space_backward, back, scaling, where):
    keep, send = terms
    chip_size, groups = lax.axis_size("dp") // 2, lax.axis_size("seq")
    rows, size = keep.shape[2:]
    count, seq_bits = chip_size.bit_length() - 1, bits_of(groups)
    keep = after(keep, *earlier)
    for step in range(count - 1):
        keep, send = halved(keep, swap_ways(send, step, count))
    order = halving(seq_bits)
    cut = (groups // 2, rows, size)
    keep, send = call(
        functools.partial(turn_kernel, order),
        [(cut, F32), (cut, BF16)],
        [((groups, rows, size), F32)],
        where,
        keep,
        swap_ways(send, count - 1, count),
        cost=SMALL,
    )
    for bit in seq_bits[:-1]:
        keep, send = halved(keep, swap(send, "seq", bit))
    keep = after(keep, back[-1])
    (total,) = halved(keep, swap(send, "seq", seq_bits[-1]))
    beside = space_backward(total)
    mine = doubled(total, count, total, beside[0], cost=SMALL)
    (whole,) = call(
        functools.partial(join_kernel, scaling),
        [((chip_size, rows, width), F32)],
        [],
        where,
        mine,
        swap(mine, "dp", 1),
        cost=SMALL,
    )
    return whole.reshape(chip_size * rows, width), beside


def divides(width):
    cuts = lax.axis_size("seq") * lax.axis_size("dp") // 2
    return width % (cuts * 8) == 0


def shards(q_space, k_space, v_space, q_time, k_time, v_time, weight, target):
    groups = lax.axis_size("seq")
    where = jnp.stack([lax.axis_index("dp"), lax.axis_index("seq")])
    rows, width = q_space.shape[1:]
    heads = width // HEAD_DIM
    per_block = rows // groups
    blocks, piece, full = (groups, per_block, width), (per_block, width), (rows, width)

    def exchange(pieces):
        return list(pieces[:1]) + [swap(pieces[i], "seq", i) for i in range(1, groups)]

    times = [item.reshape(blocks) for item in (q_time, k_time, v_time)]
    sent = call(
        functools.partial(pack_kernel, 1),
        [((3,) + piece, BF16)] * (groups - 1),
        [],
        where,
        *times,
        cost=SMALL,
    )
    (own,) = call(
        functools.partial(pack_kernel, 0),
        [((3,) + piece, BF16)],
        [],
        after(where, sent[0]),
        *times,
    )
    (rows_here,) = call(
        copy_kernel, [((1,) + weight.shape, BF16)], [], None, after(weight, sent[0])[None]
    )
    there = exchange([own, *sent])
    space = [item.reshape(full) for item in (q_space, k_space, v_space)]
    out_space, probs_s = call(
        space_forward_kernel,
        [(full, BF16), ((heads, rows, rows), F32)],
        [(full, F32)],
        None,
        *space,
    )
    full_weight = gather_weight(rows_here, (own, out_space), where)
    there[0] = after(there[0], out_space)
    outer = call(
        functools.partial(pack_kernel, 0),
        [((2,) + piece, BF16)] * groups,
        [],
        where,
        out_space.reshape(blocks),
        target.reshape(blocks),
        cost=SMALL,
    )
    probs_t, time_qkv, out_time = call(
        functools.partial(time_forward_kernel, groups),
        [((heads, rows, rows), F32), ((3,) + full, BF16), (full, F32)],
        [],
        None,
        *there,
    )
    pair, step, *steps = call(
        functools.partial(project_kernel, groups),
        [((2,) + full, BF16), (full, BF16)] + [((1,) + piece, BF16)] * groups,
        [(full, F32)],
        None,
        *exchange(outer),
        out_time,
        full_weight,
    )
    scaling = 1.0 / math.sqrt(lax.axis_size("dp") * groups * rows)
    if divides(width):
        terms = gradient_terms(pair, where)
        steps = [item if i == groups - 1 else after(item, terms[1]) for i, item in enumerate(steps)]
    (step_home,) = call(
        unpack_kernel, [(blocks, BF16)], [], where, *exchange(steps), cost=SMALL
    )
    time_grads = call(
        functools.partial(time_backward_kernel, groups),
        [((3,) + piece, BF16)] * groups,
        [(full, F32)] * 3,
        None,
        step,
        time_qkv,
        probs_t,
    )
    def space_backward(earlier):
        return call(
            space_backward_kernel,
            [(full, BF16)] * 3,
            [(full, F32)] * 3,
            None,
            *space,
            after(step_home, earlier).reshape(full),
            probs_s,
        )

    back = exchange(time_grads)
    if divides(width):
        weight_grad, space_grads = weight_gradient(
            terms, width, (time_grads[0], step_home), space_backward, back, scaling, where
        )
    else:
        term = dot(pair[0], pair[1], TN).astype(BF16)
        share = lax.psum_scatter(term, "seq", scatter_dimension=0, tiled=True)
        weight_grad = lax.psum(share, "dp").astype(F32) * scaling
        space_grads = space_backward(time_grads[0])
    back = call(unpack_kernel, [(blocks, BF16)] * 3, [], where, *back)
    outs = [item.reshape(q_space.shape) for item in list(space_grads) + list(back)]
    return tuple(outs) + (weight_grad,)


def solution(mesh):
    tokens = P("dp", "seq", None)
    return jax.shard_map(
        shards,
        mesh=mesh,
        in_specs=(tokens,) * 6 + (P("dp", None), tokens),
        out_specs=(tokens,) * 6 + (P("seq", None),),
        check_vma=False,
    )
```

```python
import functools
import math

import jax
import jax.numpy as jnp
from jax import lax
from jax.experimental import pallas as pl
from jax.experimental.pallas import tpu as pltpu
from jax.sharding import PartitionSpec as P

HEAD_DIM = 72
LANES = 128
VMEM_BYTES = 24 * 1024 * 1024
COST = 2 * 10**10
SMALL = 10
F32 = jnp.float32
BF16 = jnp.bfloat16
NT = (((1,), (1,)), ((), ()))
NN = (((1,), (0,)), ((), ()))
TN = (((0,), (0,)), ((), ()))


def dot(left, right, form):
    return lax.dot_general(left, right, form, preferred_element_type=F32)


def windows(width):
    found = []
    for head in range(width // HEAD_DIM):
        first = head * HEAD_DIM
        start = first // LANES * LANES
        size = -(-(first + HEAD_DIM - start) // LANES) * LANES
        found.append((start, size, first - start))
    return found


def head_only(block, offset):
    lane = lax.broadcasted_iota(jnp.int32, (1, block.shape[1]), 1)
    inside = (lane >= offset) & (lane < offset + HEAD_DIM)
    return jnp.where(inside, block, jnp.zeros_like(block))


def reverse(number, size):
    found = 0
    for i in range(size.bit_length() - 1):
        found = 2 * found + (number >> i & 1)
    return found


def by_core(core, even, odd):
    return even + core * (odd - even)


def same_patch(rows, per_block):
    left = lax.broadcasted_iota(jnp.int32, (rows, 1), 0) % per_block
    right = lax.broadcasted_iota(jnp.int32, (1, rows), 1) % per_block
    return left == right


def forward(per_block, q_ref, k_ref, v_ref, probs_ref, total):
    rows, width = q_ref.shape
    scaling = 1.0 / math.sqrt(HEAD_DIM)
    keep = None if per_block is None else same_patch(rows, per_block)
    total[...] = jnp.zeros_like(total)
    for head, (start, size, offset) in enumerate(windows(width)):
        lanes = slice(start, start + size)
        logits = dot(head_only(q_ref[:, lanes], offset), k_ref[:, lanes], NT) * scaling
        if keep is not None:
            logits = jnp.where(keep, logits, -1e30)
        lifted = jnp.exp(logits - jnp.max(logits, axis=-1, keepdims=True))
        probs = lifted * (1.0 / jnp.sum(lifted, axis=-1, keepdims=True))
        probs_ref[head] = probs
        total[:, lanes] += dot(probs.astype(BF16), head_only(v_ref[:, lanes], offset), NN)


def backward(q_ref, k_ref, v_ref, g_ref, probs_ref, dq_sum, dk_sum, dv_sum, heads=slice(None)):
    found = list(enumerate(windows(q_ref.shape[1])))
    for head, (start, size, offset) in found[heads]:
        lanes = slice(start, start + size)
        probs = probs_ref[head]
        step = head_only(g_ref[:, lanes], offset)
        upstream = dot(step, v_ref[:, lanes], NT)
        dv_sum[:, lanes] += dot(probs.astype(BF16), step, TN)
        mean = jnp.sum(probs * upstream, axis=-1, keepdims=True)
        dscore = (probs * (upstream - mean)).astype(BF16)
        dq_sum[:, lanes] += dot(dscore, head_only(k_ref[:, lanes], offset), NN)
        dk_sum[:, lanes] += dot(dscore, head_only(q_ref[:, lanes], offset), TN)


def space_forward_kernel(q_ref, k_ref, v_ref, out_ref, probs_ref, total):
    forward(None, q_ref, k_ref, v_ref, probs_ref, total)
    out_ref[...] = total[...].astype(BF16)


def space_first_kernel(q_ref, k_ref, v_ref, g_ref, probs_ref, *sums):
    for item in sums:
        item[...] = jnp.zeros_like(item)
    backward(q_ref, k_ref, v_ref, g_ref, probs_ref, *sums, heads=slice(probs_ref.shape[0] // 2))


def space_backward_kernel(q_ref, k_ref, v_ref, g_ref, probs_ref, *refs):
    firsts, (dq_ref, dk_ref, dv_ref), sums = refs[:3], refs[3:6], refs[6:]
    for first, item in zip(firsts, sums):
        item[...] = first[...]
    backward(
        q_ref, k_ref, v_ref, g_ref, probs_ref, *sums, heads=slice(probs_ref.shape[0] // 2, None)
    )
    scaling = 1.0 / math.sqrt(HEAD_DIM)
    dq_ref[...] = (sums[0][...] * scaling).astype(BF16)
    dk_ref[...] = (sums[1][...] * scaling).astype(BF16)
    dv_ref[...] = sums[2][...].astype(BF16)


def pack_kernel(first, where_ref, *refs):
    count = refs[-1].shape[0]
    for i, piece_ref in enumerate(refs[count:]):
        for j, array_ref in enumerate(refs[:count]):
            piece_ref[j] = array_ref[where_ref[1] ^ (first + i)]


def unpack_kernel(where_ref, *refs):
    count = refs[0].shape[0]
    groups = len(refs) - count
    for i in range(groups):
        for j in range(count):
            refs[groups + j][where_ref[1] ^ i] = refs[i][j]


def place_kernel(slots, where_ref, *refs):
    *refs, sems = refs
    pieces, outs = refs[: len(slots)], refs[-3:]
    copies = []
    for i, slot in enumerate(slots):
        for j, out_ref in enumerate(outs):
            block = out_ref.at[where_ref[1] ^ slot]
            copies.append(pltpu.make_async_copy(pieces[i].at[j], block, sems.at[i, j]))
    for copy in copies:
        copy.start()
    for copy in copies:
        copy.wait()


def time_forward_kernel(groups, *refs):
    pieces, (probs_ref, qkv_ref, total) = refs[:groups], refs[groups:]
    per_block = pieces[0].shape[1]
    for i in range(groups):
        qkv_ref[:, per_block * i : per_block * (i + 1), :] = pieces[i][...]
    forward(per_block, qkv_ref.at[0], qkv_ref.at[1], qkv_ref.at[2], probs_ref, total)


def time_backward_kernel(groups, step_ref, qkv_ref, probs_ref, *refs):
    outs, sums = refs[:groups], refs[groups:]
    per_block = outs[0].shape[1]
    for item in sums:
        item[...] = jnp.zeros_like(item)
    backward(qkv_ref.at[0], qkv_ref.at[1], qkv_ref.at[2], step_ref, probs_ref, *sums)
    scaling = 1.0 / math.sqrt(HEAD_DIM)
    for i in range(groups):
        rows = slice(per_block * i, per_block * (i + 1))
        outs[i][0] = (sums[0][rows, :] * scaling).astype(BF16)
        outs[i][1] = (sums[1][rows, :] * scaling).astype(BF16)
        outs[i][2] = sums[2][rows, :].astype(BF16)


def project_kernel(groups, *refs):
    pieces, (time_ref, weight_ref) = refs[:groups], refs[groups : groups + 2]
    pair_ref, step_ref = refs[groups + 2 : groups + 4]
    outs, total = refs[groups + 4 : 2 * groups + 4], refs[2 * groups + 4]
    per_block = pieces[0].shape[1]
    for i in range(groups):
        rows = slice(per_block * i, per_block * (i + 1))
        total[rows, :] = pieces[i][0].astype(F32) + time_ref[rows, :]
    comb = total[...].astype(BF16)
    pair_ref[0] = comb
    for i in range(groups):
        total[per_block * i : per_block * (i + 1), :] = pieces[i][1].astype(F32)
    og = (dot(comb, weight_ref[...], NN) - total[...]).astype(BF16)
    pair_ref[1] = og
    total[...] = dot(og, weight_ref[...], NT)
    step_ref[...] = total[...].astype(BF16)
    for i in range(groups):
        outs[i][0] = total[per_block * i : per_block * (i + 1), :].astype(BF16)


def copy_kernel(in_ref, out_ref):
    out_ref[...] = in_ref[...]


def stack_kernel(*refs):
    for i, ref in enumerate(refs[:-1]):
        size = ref.shape[0]
        refs[-1][i * size : (i + 1) * size] = ref[...]


def weight_kernel(where_ref, mine_ref, other_ref, out_ref):
    core, chip = where_ref[0] & 1, where_ref[0] >> 1
    size = mine_ref.shape[0]
    for i in range(size):
        back = reverse(i, size)
        out_ref[2 * (chip ^ by_core(core, i, back)) + core] = mine_ref[i]
        out_ref[2 * (chip ^ by_core(core, back, i)) + 1 - core] = other_ref[i]


def halve_kernel(keep_ref, came_ref, *outs):
    total = keep_ref[...] + came_ref[...].astype(F32)
    half = total.shape[0] // 2
    if half == 0:
        outs[0][...] = total.astype(outs[0].dtype)
    else:
        outs[0][...] = total[:half]
        outs[1][...] = total[half:].astype(BF16)


def turn_kernel(order, where_ref, mine_ref, came_ref, keep_ref, send_ref, total):
    total[...] = mine_ref[0] + came_ref[0].astype(F32)
    half = len(order) // 2
    for i, bits in enumerate(order):
        piece = total[where_ref[1] ^ bits]
        if i < half:
            keep_ref[i] = piece
        else:
            send_ref[i - half] = piece.astype(BF16)


def join_kernel(scaling, where_ref, mine_ref, other_ref, out_ref):
    core, chip = where_ref[0] & 1, where_ref[0] >> 1
    chips, _, size = mine_ref.shape
    first = core == 0
    for i in range(chips):
        back = reverse(i, chips)
        mine = mine_ref[by_core(core, i, back)].astype(F32) * scaling
        other = other_ref[by_core(core, back, i)].astype(F32) * scaling
        out_ref[chip ^ i, :, :size] = jnp.where(first, mine, other)
        out_ref[chip ^ i, :, size:] = jnp.where(first, other, mine)[:, 2 * size - out_ref.shape[-1] :]


def grad_kernel(where_ref, mine_ref, other_ref, keep_ref, send_ref, total):
    core, chip = where_ref[0] & 1, where_ref[0] >> 1
    stays, _, _, size = keep_ref.shape
    first = pl.multiple_of(core * (mine_ref.shape[-1] - size), LANES)
    term = dot(mine_ref[0], mine_ref[1, :, pl.ds(first, size)], TN)
    term += dot(other_ref[0], other_ref[1, :, pl.ds(first, size)], TN)
    total[...] = term.reshape(total.shape)
    for i in range(2 * stays):
        piece = total[:, chip ^ by_core(core, reverse(i, 2 * stays), i)]
        if i < stays:
            keep_ref[i] = piece
        else:
            send_ref[i - stays] = piece.astype(BF16)


def place(slots, pieces, arrays, shape, where):
    whole = pl.BlockSpec(memory_space=pl.ANY)
    count = len(slots)
    return pl.pallas_call(
        functools.partial(place_kernel, slots),
        out_shape=(jax.ShapeDtypeStruct(shape, BF16),) * 3,
        in_specs=[pl.BlockSpec(memory_space=pltpu.SMEM)]
        + [pl.BlockSpec(memory_space=pltpu.VMEM)] * count
        + [whole] * len(arrays),
        out_specs=(whole,) * 3,
        scratch_shapes=[pltpu.SemaphoreType.DMA((count, 3))],
        input_output_aliases={1 + count + i: i for i in range(len(arrays))},
        cost_estimate=pl.CostEstimate(flops=COST, bytes_accessed=10, transcendentals=0),
        compiler_params=pltpu.CompilerParams(vmem_limit_bytes=VMEM_BYTES),
    )(where, *pieces, *arrays)


def call(body, outs, scratch, where, *args, cost=COST):
    in_specs = [pl.BlockSpec(memory_space=pltpu.VMEM)] * len(args)
    if where is not None:
        in_specs = [pl.BlockSpec(memory_space=pltpu.SMEM)] + in_specs
        args = (where,) + args
    return pl.pallas_call(
        body,
        out_shape=tuple(jax.ShapeDtypeStruct(*out) for out in outs),
        in_specs=in_specs,
        out_specs=(pl.BlockSpec(memory_space=pltpu.VMEM),) * len(outs),
        scratch_shapes=[pltpu.VMEM(*item) for item in scratch],
        cost_estimate=pl.CostEstimate(flops=cost, bytes_accessed=10, transcendentals=0),
        compiler_params=pltpu.CompilerParams(vmem_limit_bytes=VMEM_BYTES),
    )(*args)


def swap(array, axis, bits):
    size = lax.axis_size(axis)
    return lax.ppermute(array, axis, [(i, i ^ bits) for i in range(size)])


def after(value, *others):
    return lax.optimization_barrier((value,) + others)[0]


def stack(left, right, cost=COST):
    shape = (2 * left.shape[0],) + left.shape[1:]
    return call(stack_kernel, [(shape, BF16)], [], None, left, right, cost=cost)[0]


def swap_ways(array, step, count):
    bits = (2 << step, 2 << (count - 1 - step))
    size = lax.axis_size("dp")
    return lax.ppermute(array, "dp", [(i, i ^ bits[i % 2]) for i in range(size)])


def doubled(held, count, *earlier, cost=COST):
    for step in range(count):
        came = swap_ways(held, step, count)
        if step < len(earlier):
            held = after(held, earlier[step])
        held = stack(held, came, cost)
    return held


def gather_weight(weight, earlier, where):
    size = lax.axis_size("dp")
    held = doubled(weight, (size // 2).bit_length() - 1, *earlier)
    (full,) = call(
        weight_kernel,
        [((size,) + weight.shape[1:], BF16)],
        [],
        where,
        held,
        swap(held, "dp", 1),
    )
    return full.reshape(size * weight.shape[1], weight.shape[2])


def bits_of(size):
    return [1 << i for i in range(size.bit_length() - 1)]


def halving(bits):
    order = [0]
    for bit in reversed(bits):
        order = order + [item ^ bit for item in order]
    return order


def halved(keep, came):
    count, rest = keep.shape[0], keep.shape[1:]
    if count == 1:
        return call(halve_kernel, [(keep.shape, BF16)], [], None, keep, came, cost=SMALL)
    half = (count // 2,) + rest
    return call(halve_kernel, [(half, F32), (half, BF16)], [], None, keep, came, cost=SMALL)


def gradient_terms(pair, where):
    width = pair.shape[-1]
    chip_size, groups = lax.axis_size("dp") // 2, lax.axis_size("seq")
    rows = width // groups // chip_size
    size = -(-width // (2 * LANES)) * LANES
    cut = (chip_size // 2, groups, rows, size)
    return call(
        grad_kernel,
        [(cut, F32), (cut, BF16)],
        [((groups, chip_size, rows, size), F32)],
        where,
        pair,
        swap(pair, "dp", 1),
    )


def weight_gradient(terms, width, earlier, between, space_backward, back, scaling, where):
    keep, send = terms
    chip_size, groups = lax.axis_size("dp") // 2, lax.axis_size("seq")
    rows, size = keep.shape[2:]
    count, seq_bits = chip_size.bit_length() - 1, bits_of(groups)
    keep = after(keep, *earlier)
    for step in range(count - 1):
        keep, send = halved(keep, swap_ways(send, step, count))
    order = halving(seq_bits)
    cut = (groups // 2, rows, size)
    keep, send = call(
        functools.partial(turn_kernel, order),
        [(cut, F32), (cut, BF16)],
        [((groups, rows, size), F32)],
        where,
        keep,
        swap_ways(send, count - 1, count),
        cost=SMALL,
    )
    keep = after(keep, between)
    for bit in seq_bits[:-1]:
        keep, send = halved(keep, swap(send, "seq", bit))
    keep = after(keep, back[-1])
    (total,) = halved(keep, swap(send, "seq", seq_bits[-1]))
    beside = space_backward(total)
    mine = doubled(total, count, total, beside[0], cost=SMALL)
    (whole,) = call(
        functools.partial(join_kernel, scaling),
        [((chip_size, rows, width), F32)],
        [],
        where,
        mine,
        swap(mine, "dp", 1),
        cost=SMALL,
    )
    return whole.reshape(chip_size * rows, width), beside


def divides(width):
    cuts = lax.axis_size("seq") * lax.axis_size("dp") // 2
    return width % (cuts * 8) == 0


def shards(q_space, k_space, v_space, q_time, k_time, v_time, weight, target):
    groups = lax.axis_size("seq")
    where = jnp.stack([lax.axis_index("dp"), lax.axis_index("seq")])
    rows, width = q_space.shape[1:]
    heads = width // HEAD_DIM
    per_block = rows // groups
    blocks, piece, full = (groups, per_block, width), (per_block, width), (rows, width)

    def exchange(pieces):
        return list(pieces[:1]) + [swap(pieces[i], "seq", i) for i in range(1, groups)]

    times = [item.reshape(blocks) for item in (q_time, k_time, v_time)]
    sent = call(
        functools.partial(pack_kernel, 1),
        [((3,) + piece, BF16)] * (groups - 1),
        [],
        where,
        *times,
        cost=SMALL,
    )
    (own,) = call(
        functools.partial(pack_kernel, 0),
        [((3,) + piece, BF16)],
        [],
        after(where, sent[0]),
        *times,
    )
    (rows_here,) = call(
        copy_kernel, [((1,) + weight.shape, BF16)], [], None, after(weight, sent[0])[None]
    )
    there = exchange([own, *sent])
    space = [item.reshape(full) for item in (q_space, k_space, v_space)]
    out_space, probs_s = call(
        space_forward_kernel,
        [(full, BF16), ((heads, rows, rows), F32)],
        [(full, F32)],
        None,
        *space,
    )
    full_weight = gather_weight(rows_here, (own, out_space), where)
    there[0] = after(there[0], out_space)
    outer = call(
        functools.partial(pack_kernel, 0),
        [((2,) + piece, BF16)] * groups,
        [],
        where,
        out_space.reshape(blocks),
        target.reshape(blocks),
        cost=SMALL,
    )
    probs_t, time_qkv, out_time = call(
        functools.partial(time_forward_kernel, groups),
        [((heads, rows, rows), F32), ((3,) + full, BF16), (full, F32)],
        [],
        None,
        *there,
    )
    pair, step, *steps = call(
        functools.partial(project_kernel, groups),
        [((2,) + full, BF16), (full, BF16)] + [((1,) + piece, BF16)] * groups,
        [(full, F32)],
        None,
        *exchange(outer),
        out_time,
        full_weight,
    )
    scaling = 1.0 / math.sqrt(lax.axis_size("dp") * groups * rows)
    if divides(width):
        terms = gradient_terms(pair, where)
        steps = [item if i == groups - 1 else after(item, terms[1]) for i, item in enumerate(steps)]
    steps = exchange(steps)
    (step_home,) = call(unpack_kernel, [(blocks, BF16)], [], where, *steps, cost=SMALL)
    time_grads = call(
        functools.partial(time_backward_kernel, groups),
        [((3,) + piece, BF16)] * groups,
        [(full, F32)] * 3,
        None,
        step,
        time_qkv,
        probs_t,
    )
    first_heads = call(
        space_first_kernel,
        [(full, F32)] * 3,
        [],
        None,
        *space,
        after(step_home, time_grads[0]).reshape(full),
        probs_s,
        cost=SMALL,
    )

    def space_backward(earlier):
        return call(
            space_backward_kernel,
            [(full, BF16)] * 3,
            [(full, F32)] * 3,
            None,
            *space,
            after(step_home, earlier).reshape(full),
            probs_s,
            *first_heads,
        )

    back = exchange(time_grads)
    if divides(width):
        weight_grad, space_grads = weight_gradient(
            terms, width, (time_grads[0], *steps), first_heads[0], space_backward, back, scaling, where
        )
    else:
        term = dot(pair[0], pair[1], TN).astype(BF16)
        share = lax.psum_scatter(term, "seq", scatter_dimension=0, tiled=True)
        weight_grad = lax.psum(share, "dp").astype(F32) * scaling
        space_grads = space_backward(time_grads[0])
    late = range(1, groups - 1)
    first = place([0, groups - 1], [back[0], back[-1]], [], blocks, where)
    back = place(list(late), [back[i] for i in late], first, blocks, where)
    outs = [item.reshape(q_space.shape) for item in list(space_grads) + list(back)]
    return tuple(outs) + (weight_grad,)


def solution(mesh):
    tokens = P("dp", "seq", None)
    return jax.shard_map(
        shards,
        mesh=mesh,
        in_specs=(tokens,) * 6 + (P("dp", None), tokens),
        out_specs=(tokens,) * 6 + (P("seq", None),),
        check_vma=False,
    )
```

```python
import functools
import math

import jax
import jax.numpy as jnp
from jax import lax
from jax.experimental import pallas as pl
from jax.experimental.pallas import tpu as pltpu
from jax.sharding import PartitionSpec as P

HEAD_DIM = 72
LANES = 128
VMEM_BYTES = 24 * 1024 * 1024
COST = 2 * 10**10
SMALL = 10
F32 = jnp.float32
BF16 = jnp.bfloat16
NT = (((1,), (1,)), ((), ()))
NN = (((1,), (0,)), ((), ()))
TN = (((0,), (0,)), ((), ()))


def dot(left, right, form):
    return lax.dot_general(left, right, form, preferred_element_type=F32)


def windows(width):
    found = []
    for head in range(width // HEAD_DIM):
        first = head * HEAD_DIM
        start = first // LANES * LANES
        size = -(-(first + HEAD_DIM - start) // LANES) * LANES
        found.append((start, size, first - start))
    return found


def head_only(block, offset):
    lane = lax.broadcasted_iota(jnp.int32, (1, block.shape[1]), 1)
    inside = (lane >= offset) & (lane < offset + HEAD_DIM)
    return jnp.where(inside, block, jnp.zeros_like(block))


def reverse(number, size):
    found = 0
    for i in range(size.bit_length() - 1):
        found = 2 * found + (number >> i & 1)
    return found


def by_core(core, even, odd):
    return even + core * (odd - even)


def same_patch(rows, per_block):
    left = lax.broadcasted_iota(jnp.int32, (rows, 1), 0) % per_block
    right = lax.broadcasted_iota(jnp.int32, (1, rows), 1) % per_block
    return left == right


def forward(per_block, q_ref, k_ref, v_ref, probs_ref, total):
    rows, width = q_ref.shape
    scaling = 1.0 / math.sqrt(HEAD_DIM)
    keep = None if per_block is None else same_patch(rows, per_block)
    total[...] = jnp.zeros_like(total)
    for head, (start, size, offset) in enumerate(windows(width)):
        lanes = slice(start, start + size)
        logits = dot(head_only(q_ref[:, lanes], offset), k_ref[:, lanes], NT) * scaling
        if keep is not None:
            logits = jnp.where(keep, logits, -1e30)
        lifted = jnp.exp(logits - jnp.max(logits, axis=-1, keepdims=True))
        probs = lifted * (1.0 / jnp.sum(lifted, axis=-1, keepdims=True))
        probs_ref[head] = probs
        total[:, lanes] += dot(probs.astype(BF16), head_only(v_ref[:, lanes], offset), NN)


def backward(q_ref, k_ref, v_ref, g_ref, probs_ref, dq_sum, dk_sum, dv_sum, heads=slice(None)):
    found = list(enumerate(windows(q_ref.shape[1])))
    for head, (start, size, offset) in found[heads]:
        lanes = slice(start, start + size)
        probs = probs_ref[head]
        step = head_only(g_ref[:, lanes], offset)
        upstream = dot(step, v_ref[:, lanes], NT)
        dv_sum[:, lanes] += dot(probs.astype(BF16), step, TN)
        mean = jnp.sum(probs * upstream, axis=-1, keepdims=True)
        dscore = (probs * (upstream - mean)).astype(BF16)
        dq_sum[:, lanes] += dot(dscore, head_only(k_ref[:, lanes], offset), NN)
        dk_sum[:, lanes] += dot(dscore, head_only(q_ref[:, lanes], offset), TN)


def space_forward_kernel(q_ref, k_ref, v_ref, out_ref, probs_ref, total):
    forward(None, q_ref, k_ref, v_ref, probs_ref, total)
    out_ref[...] = total[...].astype(BF16)


def space_first_kernel(q_ref, k_ref, v_ref, g_ref, probs_ref, *sums):
    for item in sums:
        item[...] = jnp.zeros_like(item)
    backward(q_ref, k_ref, v_ref, g_ref, probs_ref, *sums, heads=slice(probs_ref.shape[0] // 2))


def space_backward_kernel(q_ref, k_ref, v_ref, g_ref, probs_ref, *refs):
    firsts, (dq_ref, dk_ref, dv_ref), sums = refs[:3], refs[3:6], refs[6:]
    for first, item in zip(firsts, sums):
        item[...] = first[...]
    backward(
        q_ref, k_ref, v_ref, g_ref, probs_ref, *sums, heads=slice(probs_ref.shape[0] // 2, None)
    )
    scaling = 1.0 / math.sqrt(HEAD_DIM)
    dq_ref[...] = (sums[0][...] * scaling).astype(BF16)
    dk_ref[...] = (sums[1][...] * scaling).astype(BF16)
    dv_ref[...] = sums[2][...].astype(BF16)


def pack_kernel(first, where_ref, *refs):
    count = refs[-1].shape[0]
    for i, piece_ref in enumerate(refs[count:]):
        for j, array_ref in enumerate(refs[:count]):
            piece_ref[j] = array_ref[where_ref[1] ^ (first + i)]


def unpack_kernel(where_ref, *refs):
    count = refs[0].shape[0]
    groups = len(refs) - count
    for i in range(groups):
        for j in range(count):
            refs[groups + j][where_ref[1] ^ i] = refs[i][j]


def place_kernel(slots, where_ref, *refs):
    *refs, sems = refs
    pieces, outs = refs[: len(slots)], refs[-3:]
    copies = []
    for i, slot in enumerate(slots):
        for j, out_ref in enumerate(outs):
            block = out_ref.at[where_ref[1] ^ slot]
            copies.append(pltpu.make_async_copy(pieces[i].at[j], block, sems.at[i, j]))
    for copy in copies:
        copy.start()
    for copy in copies:
        copy.wait()


def time_forward_kernel(groups, *refs):
    pieces, (probs_ref, qkv_ref, total) = refs[:groups], refs[groups:]
    per_block = pieces[0].shape[1]
    for i in range(groups):
        qkv_ref[:, per_block * i : per_block * (i + 1), :] = pieces[i][...]
    forward(per_block, qkv_ref.at[0], qkv_ref.at[1], qkv_ref.at[2], probs_ref, total)


def time_backward_kernel(groups, step_ref, qkv_ref, probs_ref, *refs):
    outs, sums = refs[:groups], refs[groups:]
    per_block = outs[0].shape[1]
    for item in sums:
        item[...] = jnp.zeros_like(item)
    backward(qkv_ref.at[0], qkv_ref.at[1], qkv_ref.at[2], step_ref, probs_ref, *sums)
    scaling = 1.0 / math.sqrt(HEAD_DIM)
    for i in range(groups):
        rows = slice(per_block * i, per_block * (i + 1))
        outs[i][0] = (sums[0][rows, :] * scaling).astype(BF16)
        outs[i][1] = (sums[1][rows, :] * scaling).astype(BF16)
        outs[i][2] = sums[2][rows, :].astype(BF16)


def project_kernel(groups, *refs):
    pieces, (time_ref, weight_ref) = refs[:groups], refs[groups : groups + 2]
    pair_ref, step_ref = refs[groups + 2 : groups + 4]
    outs, total = refs[groups + 4 : 2 * groups + 4], refs[2 * groups + 4]
    per_block = pieces[0].shape[1]
    for i in range(groups):
        rows = slice(per_block * i, per_block * (i + 1))
        total[rows, :] = pieces[i][0].astype(F32) + time_ref[rows, :]
    comb = total[...].astype(BF16)
    pair_ref[0] = comb
    for i in range(groups):
        total[per_block * i : per_block * (i + 1), :] = pieces[i][1].astype(F32)
    og = (dot(comb, weight_ref[...], NN) - total[...]).astype(BF16)
    pair_ref[1] = og
    total[...] = dot(og, weight_ref[...], NT)
    step_ref[...] = total[...].astype(BF16)
    for i in range(groups):
        outs[i][0] = total[per_block * i : per_block * (i + 1), :].astype(BF16)


def copy_kernel(in_ref, out_ref):
    out_ref[...] = in_ref[...]


def stack_kernel(*refs):
    for i, ref in enumerate(refs[:-1]):
        size = ref.shape[0]
        refs[-1][i * size : (i + 1) * size] = ref[...]


def weight_kernel(where_ref, mine_ref, other_ref, out_ref):
    core, chip = where_ref[0] & 1, where_ref[0] >> 1
    size = mine_ref.shape[0]
    for i in range(size):
        back = reverse(i, size)
        out_ref[2 * (chip ^ by_core(core, i, back)) + core] = mine_ref[i]
        out_ref[2 * (chip ^ by_core(core, back, i)) + 1 - core] = other_ref[i]


def halve_kernel(keep_ref, came_ref, *outs):
    total = keep_ref[...] + came_ref[...].astype(F32)
    half = total.shape[0] // 2
    if half == 0:
        outs[0][...] = total.astype(outs[0].dtype)
    else:
        outs[0][...] = total[:half]
        outs[1][...] = total[half:].astype(BF16)


def turn_kernel(order, where_ref, mine_ref, came_ref, keep_ref, send_ref, total):
    total[...] = mine_ref[0] + came_ref[0].astype(F32)
    half = len(order) // 2
    for i, bits in enumerate(order):
        piece = total[where_ref[1] ^ bits]
        if i < half:
            keep_ref[i] = piece
        else:
            send_ref[i - half] = piece.astype(BF16)


def join_kernel(scaling, where_ref, mine_ref, other_ref, out_ref):
    core, chip = where_ref[0] & 1, where_ref[0] >> 1
    chips, _, size = mine_ref.shape
    first = core == 0
    for i in range(chips):
        back = reverse(i, chips)
        mine = mine_ref[by_core(core, i, back)].astype(F32) * scaling
        other = other_ref[by_core(core, back, i)].astype(F32) * scaling
        out_ref[chip ^ i, :, :size] = jnp.where(first, mine, other)
        out_ref[chip ^ i, :, size:] = jnp.where(first, other, mine)[:, 2 * size - out_ref.shape[-1] :]


def grad_kernel(where_ref, mine_ref, other_ref, keep_ref, send_ref, total):
    core, chip = where_ref[0] & 1, where_ref[0] >> 1
    stays, _, _, size = keep_ref.shape
    first = pl.multiple_of(core * (mine_ref.shape[-1] - size), LANES)
    term = dot(mine_ref[0], mine_ref[1, :, pl.ds(first, size)], TN)
    term += dot(other_ref[0], other_ref[1, :, pl.ds(first, size)], TN)
    total[...] = term.reshape(total.shape)
    for i in range(2 * stays):
        piece = total[:, chip ^ by_core(core, reverse(i, 2 * stays), i)]
        if i < stays:
            keep_ref[i] = piece
        else:
            send_ref[i - stays] = piece.astype(BF16)


def place(slots, pieces, arrays, shape, where):
    whole = pl.BlockSpec(memory_space=pl.ANY)
    count = len(slots)
    return pl.pallas_call(
        functools.partial(place_kernel, slots),
        out_shape=(jax.ShapeDtypeStruct(shape, BF16),) * 3,
        in_specs=[pl.BlockSpec(memory_space=pltpu.SMEM)]
        + [pl.BlockSpec(memory_space=pltpu.VMEM)] * count
        + [whole] * len(arrays),
        out_specs=(whole,) * 3,
        scratch_shapes=[pltpu.SemaphoreType.DMA((count, 3))],
        input_output_aliases={1 + count + i: i for i in range(len(arrays))},
        cost_estimate=pl.CostEstimate(flops=COST, bytes_accessed=10, transcendentals=0),
        compiler_params=pltpu.CompilerParams(vmem_limit_bytes=VMEM_BYTES),
    )(where, *pieces, *arrays)


def call(body, outs, scratch, where, *args, cost=COST):
    in_specs = [pl.BlockSpec(memory_space=pltpu.VMEM)] * len(args)
    if where is not None:
        in_specs = [pl.BlockSpec(memory_space=pltpu.SMEM)] + in_specs
        args = (where,) + args
    return pl.pallas_call(
        body,
        out_shape=tuple(jax.ShapeDtypeStruct(*out) for out in outs),
        in_specs=in_specs,
        out_specs=(pl.BlockSpec(memory_space=pltpu.VMEM),) * len(outs),
        scratch_shapes=[pltpu.VMEM(*item) for item in scratch],
        cost_estimate=pl.CostEstimate(flops=cost, bytes_accessed=10, transcendentals=0),
        compiler_params=pltpu.CompilerParams(vmem_limit_bytes=VMEM_BYTES),
    )(*args)


def swap(array, axis, bits):
    size = lax.axis_size(axis)
    return lax.ppermute(array, axis, [(i, i ^ bits) for i in range(size)])


def after(value, *others):
    return lax.optimization_barrier((value,) + others)[0]


def stack(left, right, cost=COST):
    shape = (2 * left.shape[0],) + left.shape[1:]
    return call(stack_kernel, [(shape, BF16)], [], None, left, right, cost=cost)[0]


def swap_ways(array, step, count):
    bits = (2 << step, 2 << (count - 1 - step))
    size = lax.axis_size("dp")
    return lax.ppermute(array, "dp", [(i, i ^ bits[i % 2]) for i in range(size)])


def doubled(held, count, *earlier, cost=COST):
    for step in range(count):
        came = swap_ways(held, step, count)
        if step < len(earlier):
            held = after(held, earlier[step])
        held = stack(held, came, cost)
    return held


def gather_weight(weight, earlier, where):
    size = lax.axis_size("dp")
    held = doubled(weight, (size // 2).bit_length() - 1, *earlier)
    (full,) = call(
        weight_kernel,
        [((size,) + weight.shape[1:], BF16)],
        [],
        where,
        held,
        swap(held, "dp", 1),
    )
    return full.reshape(size * weight.shape[1], weight.shape[2])


def bits_of(size):
    return [1 << i for i in range(size.bit_length() - 1)]


def halving(bits):
    order = [0]
    for bit in reversed(bits):
        order = order + [item ^ bit for item in order]
    return order


def halved(keep, came):
    count, rest = keep.shape[0], keep.shape[1:]
    if count == 1:
        return call(halve_kernel, [(keep.shape, BF16)], [], None, keep, came, cost=SMALL)
    half = (count // 2,) + rest
    return call(halve_kernel, [(half, F32), (half, BF16)], [], None, keep, came, cost=SMALL)


def gradient_terms(pair, where):
    width = pair.shape[-1]
    chip_size, groups = lax.axis_size("dp") // 2, lax.axis_size("seq")
    rows = width // groups // chip_size
    size = -(-width // (2 * LANES)) * LANES
    cut = (chip_size // 2, groups, rows, size)
    return call(
        grad_kernel,
        [(cut, F32), (cut, BF16)],
        [((groups, chip_size, rows, size), F32)],
        where,
        pair,
        swap(pair, "dp", 1),
    )


def weight_gradient(terms, width, earlier, between, space_backward, back, scaling, where):
    keep, send = terms
    chip_size, groups = lax.axis_size("dp") // 2, lax.axis_size("seq")
    rows, size = keep.shape[2:]
    count, seq_bits = chip_size.bit_length() - 1, bits_of(groups)
    keep = after(keep, *earlier)
    for step in range(count - 1):
        keep, send = halved(keep, swap_ways(send, step, count))
    keep = after(keep, between)
    order = halving(seq_bits)
    cut = (groups // 2, rows, size)
    keep, send = call(
        functools.partial(turn_kernel, order),
        [(cut, F32), (cut, BF16)],
        [((groups, rows, size), F32)],
        where,
        keep,
        swap_ways(send, count - 1, count),
        cost=SMALL,
    )
    for bit in seq_bits[:-1]:
        keep, send = halved(keep, swap(send, "seq", bit))
    keep = after(keep, back[-1])
    (total,) = halved(keep, swap(send, "seq", seq_bits[-1]))
    beside = space_backward(total)
    mine = doubled(total, count, total, beside[0], cost=SMALL)
    (whole,) = call(
        functools.partial(join_kernel, scaling),
        [((chip_size, rows, width), F32)],
        [],
        where,
        mine,
        swap(mine, "dp", 1),
        cost=SMALL,
    )
    return whole.reshape(chip_size * rows, width), beside


def divides(width):
    cuts = lax.axis_size("seq") * lax.axis_size("dp") // 2
    return width % (cuts * 8) == 0


def shards(q_space, k_space, v_space, q_time, k_time, v_time, weight, target):
    groups = lax.axis_size("seq")
    where = jnp.stack([lax.axis_index("dp"), lax.axis_index("seq")])
    rows, width = q_space.shape[1:]
    heads = width // HEAD_DIM
    per_block = rows // groups
    blocks, piece, full = (groups, per_block, width), (per_block, width), (rows, width)

    def exchange(pieces):
        return list(pieces[:1]) + [swap(pieces[i], "seq", i) for i in range(1, groups)]

    times = [item.reshape(blocks) for item in (q_time, k_time, v_time)]
    sent = call(
        functools.partial(pack_kernel, 1),
        [((3,) + piece, BF16)] * (groups - 1),
        [],
        where,
        *times,
        cost=SMALL,
    )
    (own,) = call(
        functools.partial(pack_kernel, 0),
        [((3,) + piece, BF16)],
        [],
        after(where, sent[0]),
        *times,
    )
    (rows_here,) = call(
        copy_kernel, [((1,) + weight.shape, BF16)], [], None, after(weight, sent[0])[None]
    )
    there = exchange([own, *sent])
    space = [item.reshape(full) for item in (q_space, k_space, v_space)]
    out_space, probs_s = call(
        space_forward_kernel,
        [(full, BF16), ((heads, rows, rows), F32)],
        [(full, F32)],
        None,
        *space,
    )
    full_weight = gather_weight(rows_here, (own, out_space), where)
    there[0] = after(there[0], out_space)
    outer = call(
        functools.partial(pack_kernel, 0),
        [((2,) + piece, BF16)] * groups,
        [],
        where,
        out_space.reshape(blocks),
        target.reshape(blocks),
        cost=SMALL,
    )
    probs_t, time_qkv, out_time = call(
        functools.partial(time_forward_kernel, groups),
        [((heads, rows, rows), F32), ((3,) + full, BF16), (full, F32)],
        [],
        None,
        *there,
    )
    pair, step, *steps = call(
        functools.partial(project_kernel, groups),
        [((2,) + full, BF16), (full, BF16)] + [((1,) + piece, BF16)] * groups,
        [(full, F32)],
        None,
        *exchange(outer),
        out_time,
        full_weight,
    )
    scaling = 1.0 / math.sqrt(lax.axis_size("dp") * groups * rows)
    if divides(width):
        terms = gradient_terms(pair, where)
        steps = [item if i == groups - 1 else after(item, terms[1]) for i, item in enumerate(steps)]
    steps = exchange(steps)
    (step_home,) = call(unpack_kernel, [(blocks, BF16)], [], where, *steps, cost=SMALL)
    time_grads = call(
        functools.partial(time_backward_kernel, groups),
        [((3,) + piece, BF16)] * groups,
        [(full, F32)] * 3,
        None,
        step,
        time_qkv,
        probs_t,
    )
    first_heads = call(
        space_first_kernel,
        [(full, F32)] * 3,
        [],
        None,
        *space,
        after(step_home, time_grads[0]).reshape(full),
        probs_s,
        cost=SMALL,
    )

    def space_backward(earlier):
        return call(
            space_backward_kernel,
            [(full, BF16)] * 3,
            [(full, F32)] * 3,
            None,
            *space,
            after(step_home, earlier).reshape(full),
            probs_s,
            *first_heads,
        )

    back = exchange(time_grads)
    if divides(width):
        weight_grad, space_grads = weight_gradient(
            terms, width, (time_grads[0], *steps), first_heads[0], space_backward, back, scaling, where
        )
    else:
        term = dot(pair[0], pair[1], TN).astype(BF16)
        share = lax.psum_scatter(term, "seq", scatter_dimension=0, tiled=True)
        weight_grad = lax.psum(share, "dp").astype(F32) * scaling
        space_grads = space_backward(time_grads[0])
    late = range(1, groups - 1)
    first = place([0, groups - 1], [back[0], back[-1]], [], blocks, where)
    back = place(list(late), [back[i] for i in late], first, blocks, where)
    outs = [item.reshape(q_space.shape) for item in list(space_grads) + list(back)]
    return tuple(outs) + (weight_grad,)


def solution(mesh):
    tokens = P("dp", "seq", None)
    return jax.shard_map(
        shards,
        mesh=mesh,
        in_specs=(tokens,) * 6 + (P("dp", None), tokens),
        out_specs=(tokens,) * 6 + (P("seq", None),),
        check_vma=False,
    )
```

```python
import functools
import math

import jax
import jax.numpy as jnp
from jax import lax
from jax.experimental import pallas as pl
from jax.experimental.pallas import tpu as pltpu
from jax.sharding import PartitionSpec as P

HEAD_DIM = 72
LANES = 128
VMEM_BYTES = 24 * 1024 * 1024
COST = 2 * 10**10
SMALL = 10
F32 = jnp.float32
BF16 = jnp.bfloat16
NT = (((1,), (1,)), ((), ()))
NN = (((1,), (0,)), ((), ()))
TN = (((0,), (0,)), ((), ()))


def dot(left, right, form):
    return lax.dot_general(left, right, form, preferred_element_type=F32)


def windows(width):
    found = []
    for head in range(width // HEAD_DIM):
        first = head * HEAD_DIM
        start = first // LANES * LANES
        size = -(-(first + HEAD_DIM - start) // LANES) * LANES
        found.append((start, size, first - start))
    return found


def head_only(block, offset):
    lane = lax.broadcasted_iota(jnp.int32, (1, block.shape[1]), 1)
    inside = (lane >= offset) & (lane < offset + HEAD_DIM)
    return jnp.where(inside, block, jnp.zeros_like(block))


def reverse(number, size):
    found = 0
    for i in range(size.bit_length() - 1):
        found = 2 * found + (number >> i & 1)
    return found


def by_core(core, even, odd):
    return even + core * (odd - even)


def same_patch(rows, per_block):
    left = lax.broadcasted_iota(jnp.int32, (rows, 1), 0) % per_block
    right = lax.broadcasted_iota(jnp.int32, (1, rows), 1) % per_block
    return left == right


def forward(per_block, q_ref, k_ref, v_ref, probs_ref, total):
    rows, width = q_ref.shape
    scaling = 1.0 / math.sqrt(HEAD_DIM)
    keep = None if per_block is None else same_patch(rows, per_block)
    total[...] = jnp.zeros_like(total)
    for head, (start, size, offset) in enumerate(windows(width)):
        lanes = slice(start, start + size)
        logits = dot(head_only(q_ref[:, lanes], offset), k_ref[:, lanes], NT) * scaling
        if keep is not None:
            logits = jnp.where(keep, logits, -1e30)
        lifted = jnp.exp(logits - jnp.max(logits, axis=-1, keepdims=True))
        probs = lifted * (1.0 / jnp.sum(lifted, axis=-1, keepdims=True))
        probs_ref[head] = probs
        total[:, lanes] += dot(probs.astype(BF16), head_only(v_ref[:, lanes], offset), NN)


def backward(q_ref, k_ref, v_ref, g_ref, probs_ref, dq_sum, dk_sum, dv_sum, heads=slice(None)):
    found = list(enumerate(windows(q_ref.shape[1])))
    for head, (start, size, offset) in found[heads]:
        lanes = slice(start, start + size)
        probs = probs_ref[head]
        step = head_only(g_ref[:, lanes], offset)
        upstream = dot(step, v_ref[:, lanes], NT)
        dv_sum[:, lanes] += dot(probs.astype(BF16), step, TN)
        mean = jnp.sum(probs * upstream, axis=-1, keepdims=True)
        dscore = (probs * (upstream - mean)).astype(BF16)
        dq_sum[:, lanes] += dot(dscore, head_only(k_ref[:, lanes], offset), NN)
        dk_sum[:, lanes] += dot(dscore, head_only(q_ref[:, lanes], offset), TN)


def space_forward_kernel(q_ref, k_ref, v_ref, out_ref, probs_ref, total):
    forward(None, q_ref, k_ref, v_ref, probs_ref, total)
    out_ref[...] = total[...].astype(BF16)


def space_first_kernel(q_ref, k_ref, v_ref, g_ref, probs_ref, *sums):
    for item in sums:
        item[...] = jnp.zeros_like(item)
    backward(q_ref, k_ref, v_ref, g_ref, probs_ref, *sums, heads=slice(probs_ref.shape[0] * 5 // 8))


def space_backward_kernel(q_ref, k_ref, v_ref, g_ref, probs_ref, *refs):
    firsts, (dq_ref, dk_ref, dv_ref), sums = refs[:3], refs[3:6], refs[6:]
    for first, item in zip(firsts, sums):
        item[...] = first[...]
    backward(
        q_ref, k_ref, v_ref, g_ref, probs_ref, *sums, heads=slice(probs_ref.shape[0] * 5 // 8, None)
    )
    scaling = 1.0 / math.sqrt(HEAD_DIM)
    dq_ref[...] = (sums[0][...] * scaling).astype(BF16)
    dk_ref[...] = (sums[1][...] * scaling).astype(BF16)
    dv_ref[...] = sums[2][...].astype(BF16)


def pack_kernel(first, where_ref, *refs):
    count = refs[-1].shape[0]
    for i, piece_ref in enumerate(refs[count:]):
        for j, array_ref in enumerate(refs[:count]):
            piece_ref[j] = array_ref[where_ref[1] ^ (first + i)]


def unpack_kernel(where_ref, *refs):
    count = refs[0].shape[0]
    groups = len(refs) - count
    for i in range(groups):
        for j in range(count):
            refs[groups + j][where_ref[1] ^ i] = refs[i][j]


def place_kernel(slots, where_ref, *refs):
    *refs, sems = refs
    pieces, outs = refs[: len(slots)], refs[-3:]
    copies = []
    for i, slot in enumerate(slots):
        for j, out_ref in enumerate(outs):
            block = out_ref.at[where_ref[1] ^ slot]
            copies.append(pltpu.make_async_copy(pieces[i].at[j], block, sems.at[i, j]))
    for copy in copies:
        copy.start()
    for copy in copies:
        copy.wait()


def time_forward_kernel(groups, *refs):
    pieces, (probs_ref, qkv_ref, total) = refs[:groups], refs[groups:]
    per_block = pieces[0].shape[1]
    for i in range(groups):
        qkv_ref[:, per_block * i : per_block * (i + 1), :] = pieces[i][...]
    forward(per_block, qkv_ref.at[0], qkv_ref.at[1], qkv_ref.at[2], probs_ref, total)


def time_backward_kernel(groups, step_ref, qkv_ref, probs_ref, *refs):
    outs, sums = refs[:groups], refs[groups:]
    per_block = outs[0].shape[1]
    for item in sums:
        item[...] = jnp.zeros_like(item)
    backward(qkv_ref.at[0], qkv_ref.at[1], qkv_ref.at[2], step_ref, probs_ref, *sums)
    scaling = 1.0 / math.sqrt(HEAD_DIM)
    for i in range(groups):
        rows = slice(per_block * i, per_block * (i + 1))
        outs[i][0] = (sums[0][rows, :] * scaling).astype(BF16)
        outs[i][1] = (sums[1][rows, :] * scaling).astype(BF16)
        outs[i][2] = sums[2][rows, :].astype(BF16)


def project_kernel(groups, *refs):
    pieces, (time_ref, weight_ref) = refs[:groups], refs[groups : groups + 2]
    pair_ref, step_ref = refs[groups + 2 : groups + 4]
    outs, total = refs[groups + 4 : 2 * groups + 4], refs[2 * groups + 4]
    per_block = pieces[0].shape[1]
    for i in range(groups):
        rows = slice(per_block * i, per_block * (i + 1))
        total[rows, :] = pieces[i][0].astype(F32) + time_ref[rows, :]
    comb = total[...].astype(BF16)
    pair_ref[0] = comb
    for i in range(groups):
        total[per_block * i : per_block * (i + 1), :] = pieces[i][1].astype(F32)
    og = (dot(comb, weight_ref[...], NN) - total[...]).astype(BF16)
    pair_ref[1] = og
    total[...] = dot(og, weight_ref[...], NT)
    step_ref[...] = total[...].astype(BF16)
    for i in range(groups):
        outs[i][0] = total[per_block * i : per_block * (i + 1), :].astype(BF16)


def copy_kernel(in_ref, out_ref):
    out_ref[...] = in_ref[...]


def stack_kernel(*refs):
    for i, ref in enumerate(refs[:-1]):
        size = ref.shape[0]
        refs[-1][i * size : (i + 1) * size] = ref[...]


def weight_kernel(where_ref, mine_ref, other_ref, out_ref):
    core, chip = where_ref[0] & 1, where_ref[0] >> 1
    size = mine_ref.shape[0]
    for i in range(size):
        back = reverse(i, size)
        out_ref[2 * (chip ^ by_core(core, i, back)) + core] = mine_ref[i]
        out_ref[2 * (chip ^ by_core(core, back, i)) + 1 - core] = other_ref[i]


def halve_kernel(keep_ref, came_ref, *outs):
    total = keep_ref[...] + came_ref[...].astype(F32)
    half = total.shape[0] // 2
    if half == 0:
        outs[0][...] = total.astype(outs[0].dtype)
    else:
        outs[0][...] = total[:half]
        outs[1][...] = total[half:].astype(BF16)


def turn_kernel(order, where_ref, mine_ref, came_ref, keep_ref, send_ref, total):
    total[...] = mine_ref[0] + came_ref[0].astype(F32)
    half = len(order) // 2
    for i, bits in enumerate(order):
        piece = total[where_ref[1] ^ bits]
        if i < half:
            keep_ref[i] = piece
        else:
            send_ref[i - half] = piece.astype(BF16)


def join_kernel(scaling, where_ref, mine_ref, other_ref, out_ref):
    core, chip = where_ref[0] & 1, where_ref[0] >> 1
    chips, _, size = mine_ref.shape
    first = core == 0
    for i in range(chips):
        back = reverse(i, chips)
        mine = mine_ref[by_core(core, i, back)].astype(F32) * scaling
        other = other_ref[by_core(core, back, i)].astype(F32) * scaling
        out_ref[chip ^ i, :, :size] = jnp.where(first, mine, other)
        out_ref[chip ^ i, :, size:] = jnp.where(first, other, mine)[:, 2 * size - out_ref.shape[-1] :]


def grad_kernel(where_ref, mine_ref, other_ref, keep_ref, send_ref, total):
    core, chip = where_ref[0] & 1, where_ref[0] >> 1
    stays, _, _, size = keep_ref.shape
    first = pl.multiple_of(core * (mine_ref.shape[-1] - size), LANES)
    term = dot(mine_ref[0], mine_ref[1, :, pl.ds(first, size)], TN)
    term += dot(other_ref[0], other_ref[1, :, pl.ds(first, size)], TN)
    total[...] = term.reshape(total.shape)
    for i in range(2 * stays):
        piece = total[:, chip ^ by_core(core, reverse(i, 2 * stays), i)]
        if i < stays:
            keep_ref[i] = piece
        else:
            send_ref[i - stays] = piece.astype(BF16)


def place(slots, pieces, arrays, shape, where):
    whole = pl.BlockSpec(memory_space=pl.ANY)
    count = len(slots)
    return pl.pallas_call(
        functools.partial(place_kernel, slots),
        out_shape=(jax.ShapeDtypeStruct(shape, BF16),) * 3,
        in_specs=[pl.BlockSpec(memory_space=pltpu.SMEM)]
        + [pl.BlockSpec(memory_space=pltpu.VMEM)] * count
        + [whole] * len(arrays),
        out_specs=(whole,) * 3,
        scratch_shapes=[pltpu.SemaphoreType.DMA((count, 3))],
        input_output_aliases={1 + count + i: i for i in range(len(arrays))},
        cost_estimate=pl.CostEstimate(flops=COST, bytes_accessed=10, transcendentals=0),
        compiler_params=pltpu.CompilerParams(vmem_limit_bytes=VMEM_BYTES),
    )(where, *pieces, *arrays)


def call(body, outs, scratch, where, *args, cost=COST):
    in_specs = [pl.BlockSpec(memory_space=pltpu.VMEM)] * len(args)
    if where is not None:
        in_specs = [pl.BlockSpec(memory_space=pltpu.SMEM)] + in_specs
        args = (where,) + args
    return pl.pallas_call(
        body,
        out_shape=tuple(jax.ShapeDtypeStruct(*out) for out in outs),
        in_specs=in_specs,
        out_specs=(pl.BlockSpec(memory_space=pltpu.VMEM),) * len(outs),
        scratch_shapes=[pltpu.VMEM(*item) for item in scratch],
        cost_estimate=pl.CostEstimate(flops=cost, bytes_accessed=10, transcendentals=0),
        compiler_params=pltpu.CompilerParams(vmem_limit_bytes=VMEM_BYTES),
    )(*args)


def swap(array, axis, bits):
    size = lax.axis_size(axis)
    return lax.ppermute(array, axis, [(i, i ^ bits) for i in range(size)])


def after(value, *others):
    return lax.optimization_barrier((value,) + others)[0]


def stack(left, right, cost=COST):
    shape = (2 * left.shape[0],) + left.shape[1:]
    return call(stack_kernel, [(shape, BF16)], [], None, left, right, cost=cost)[0]


def swap_ways(array, step, count):
    bits = (2 << step, 2 << (count - 1 - step))
    size = lax.axis_size("dp")
    return lax.ppermute(array, "dp", [(i, i ^ bits[i % 2]) for i in range(size)])


def doubled(held, count, *earlier, cost=COST):
    for step in range(count):
        came = swap_ways(held, step, count)
        if step < len(earlier):
            held = after(held, earlier[step])
        held = stack(held, came, cost)
    return held


def gather_weight(weight, earlier, where):
    size = lax.axis_size("dp")
    held = doubled(weight, (size // 2).bit_length() - 1, *earlier)
    (full,) = call(
        weight_kernel,
        [((size,) + weight.shape[1:], BF16)],
        [],
        where,
        held,
        swap(held, "dp", 1),
    )
    return full.reshape(size * weight.shape[1], weight.shape[2])


def bits_of(size):
    return [1 << i for i in range(size.bit_length() - 1)]


def halving(bits):
    order = [0]
    for bit in reversed(bits):
        order = order + [item ^ bit for item in order]
    return order


def halved(keep, came):
    count, rest = keep.shape[0], keep.shape[1:]
    if count == 1:
        return call(halve_kernel, [(keep.shape, BF16)], [], None, keep, came, cost=SMALL)
    half = (count // 2,) + rest
    return call(halve_kernel, [(half, F32), (half, BF16)], [], None, keep, came, cost=SMALL)


def gradient_terms(pair, where):
    width = pair.shape[-1]
    chip_size, groups = lax.axis_size("dp") // 2, lax.axis_size("seq")
    rows = width // groups // chip_size
    size = -(-width // (2 * LANES)) * LANES
    cut = (chip_size // 2, groups, rows, size)
    return call(
        grad_kernel,
        [(cut, F32), (cut, BF16)],
        [((groups, chip_size, rows, size), F32)],
        where,
        pair,
        swap(pair, "dp", 1),
    )


def weight_gradient(terms, width, earlier, between, space_backward, back, scaling, where):
    keep, send = terms
    chip_size, groups = lax.axis_size("dp") // 2, lax.axis_size("seq")
    rows, size = keep.shape[2:]
    count, seq_bits = chip_size.bit_length() - 1, bits_of(groups)
    keep = after(keep, *earlier)
    for step in range(count - 1):
        keep, send = halved(keep, swap_ways(send, step, count))
    order = halving(seq_bits)
    cut = (groups // 2, rows, size)
    keep, send = call(
        functools.partial(turn_kernel, order),
        [(cut, F32), (cut, BF16)],
        [((groups, rows, size), F32)],
        where,
        keep,
        swap_ways(send, count - 1, count),
        cost=SMALL,
    )
    keep = after(keep, between)
    for bit in seq_bits[:-1]:
        keep, send = halved(keep, swap(send, "seq", bit))
    keep = after(keep, back[-1])
    (total,) = halved(keep, swap(send, "seq", seq_bits[-1]))
    beside = space_backward(total)
    mine = doubled(total, count, total, beside[0], cost=SMALL)
    (whole,) = call(
        functools.partial(join_kernel, scaling),
        [((chip_size, rows, width), F32)],
        [],
        where,
        mine,
        swap(mine, "dp", 1),
        cost=SMALL,
    )
    return whole.reshape(chip_size * rows, width), beside


def divides(width):
    cuts = lax.axis_size("seq") * lax.axis_size("dp") // 2
    return width % (cuts * 8) == 0


def shards(q_space, k_space, v_space, q_time, k_time, v_time, weight, target):
    groups = lax.axis_size("seq")
    where = jnp.stack([lax.axis_index("dp"), lax.axis_index("seq")])
    rows, width = q_space.shape[1:]
    heads = width // HEAD_DIM
    per_block = rows // groups
    blocks, piece, full = (groups, per_block, width), (per_block, width), (rows, width)

    def exchange(pieces):
        return list(pieces[:1]) + [swap(pieces[i], "seq", i) for i in range(1, groups)]

    times = [item.reshape(blocks) for item in (q_time, k_time, v_time)]
    sent = call(
        functools.partial(pack_kernel, 1),
        [((3,) + piece, BF16)] * (groups - 1),
        [],
        where,
        *times,
        cost=SMALL,
    )
    (own,) = call(
        functools.partial(pack_kernel, 0),
        [((3,) + piece, BF16)],
        [],
        after(where, sent[0]),
        *times,
    )
    (rows_here,) = call(
        copy_kernel, [((1,) + weight.shape, BF16)], [], None, after(weight, sent[0])[None]
    )
    there = exchange([own, *sent])
    space = [item.reshape(full) for item in (q_space, k_space, v_space)]
    out_space, probs_s = call(
        space_forward_kernel,
        [(full, BF16), ((heads, rows, rows), F32)],
        [(full, F32)],
        None,
        *space,
    )
    full_weight = gather_weight(rows_here, (own, out_space), where)
    there[0] = after(there[0], out_space)
    outer = call(
        functools.partial(pack_kernel, 0),
        [((2,) + piece, BF16)] * groups,
        [],
        where,
        out_space.reshape(blocks),
        target.reshape(blocks),
        cost=SMALL,
    )
    probs_t, time_qkv, out_time = call(
        functools.partial(time_forward_kernel, groups),
        [((heads, rows, rows), F32), ((3,) + full, BF16), (full, F32)],
        [],
        None,
        *there,
    )
    pair, step, *steps = call(
        functools.partial(project_kernel, groups),
        [((2,) + full, BF16), (full, BF16)] + [((1,) + piece, BF16)] * groups,
        [(full, F32)],
        None,
        *exchange(outer),
        out_time,
        full_weight,
    )
    scaling = 1.0 / math.sqrt(lax.axis_size("dp") * groups * rows)
    if divides(width):
        terms = gradient_terms(pair, where)
        steps = [item if i == groups - 1 else after(item, terms[1]) for i, item in enumerate(steps)]
    steps = exchange(steps)
    (step_home,) = call(unpack_kernel, [(blocks, BF16)], [], where, *steps, cost=SMALL)
    time_grads = call(
        functools.partial(time_backward_kernel, groups),
        [((3,) + piece, BF16)] * groups,
        [(full, F32)] * 3,
        None,
        step,
        time_qkv,
        probs_t,
    )
    first_heads = call(
        space_first_kernel,
        [(full, F32)] * 3,
        [],
        None,
        *space,
        after(step_home, time_grads[0]).reshape(full),
        probs_s,
        cost=SMALL,
    )

    def space_backward(earlier):
        return call(
            space_backward_kernel,
            [(full, BF16)] * 3,
            [(full, F32)] * 3,
            None,
            *space,
            after(step_home, earlier).reshape(full),
            probs_s,
            *first_heads,
        )

    back = exchange(time_grads)
    if divides(width):
        weight_grad, space_grads = weight_gradient(
            terms, width, (time_grads[0], *steps), first_heads[0], space_backward, back, scaling, where
        )
    else:
        term = dot(pair[0], pair[1], TN).astype(BF16)
        share = lax.psum_scatter(term, "seq", scatter_dimension=0, tiled=True)
        weight_grad = lax.psum(share, "dp").astype(F32) * scaling
        space_grads = space_backward(time_grads[0])
    late = range(1, groups - 1)
    first = place([0, groups - 1], [back[0], back[-1]], [], blocks, where)
    back = place(list(late), [back[i] for i in late], first, blocks, where)
    outs = [item.reshape(q_space.shape) for item in list(space_grads) + list(back)]
    return tuple(outs) + (weight_grad,)


def solution(mesh):
    tokens = P("dp", "seq", None)
    return jax.shard_map(
        shards,
        mesh=mesh,
        in_specs=(tokens,) * 6 + (P("dp", None), tokens),
        out_specs=(tokens,) * 6 + (P("seq", None),),
        check_vma=False,
    )
```
